256 devices in a mesh: expert: 128 (over y, x, z), rep: 2 (over core).
Axes of the slice: x: 4, y: 4, z: 8, core: 2. Of those that a mesh axis runs over, the one named last changes fastest.
Arguments:
- inputs: bfloat16 [32768, 2048], P(('expert', 'rep')), may hold values from -6 to 6
- out_grad: bfloat16 [32768, 2048], P(('expert', 'rep')), may hold values from -3 to 3
- expert_ids: int32 [32768, 2], P(('expert', 'rep')), may hold values from 0 to 127, all different within a row; in each aligned block of 128 rows (0 to 127, 128 to 255, ...) at most 4 rows name the same one
- gates: float32 [32768, 2], P(('expert', 'rep')), may hold values from 0.1 to 1
- gate_w: bfloat16 [128, 2048, 768], P('expert', 'rep'), may hold values from -0.125 to 0.125
- up_w: bfloat16 [128, 2048, 768], P('expert', 'rep'), may hold values from -0.125 to 0.125
- down_w: bfloat16 [128, 768, 2048], P('expert', None, 'rep'), may hold values from -0.21875 to 0.21875
Outputs:
- input_grad: bfloat16 [32768, 2048], P(('expert', 'rep'))
- gate_w_grad: bfloat16 [128, 2048, 768], P('expert', 'rep')
- up_w_grad: bfloat16 [128, 2048, 768], P('expert', 'rep')
- down_w_grad: bfloat16 [128, 768, 2048], P('expert', None, 'rep')
The draws below stay inside these ranges and needn't reach their ends.
Inputs may be any that keep to these rules, and one draw needn't show every extreme that they name: `expert_ids`: each row names 2 different experts; within the 128 rows of one device no expert is named more than 4 times.
All inputs are finite; a program needn't handle non-finite values.
Results may differ from the reference program's by a relative error of at most 0.0065.
Values may be sent and summed in bfloat16 or wider, within the bound.
No kernel may reach another device: no remote copies, remote signals or barrier semaphores. Data moves between devices by JAX's collectives and lax.ppermute only.
A program may use at most 128 MiB of HBM per device.

```python
import math
import jax
import jax.numpy as jnp
import numpy as np
from jax import lax

D = 2048
H = 768
TOPK = 2
TOK_DEV = 128
EXPERTS = 128
GROUPS = 128
REPLICAS = 2
CAP = 4
TOKENS = 32768


def level_of(own_key, dims, pieces, least, high):
    def one(dim, blocks):
        heights = jax.random.uniform(jax.random.fold_in(jax.random.fold_in(own_key, 6), dim), (blocks,), jnp.float32, least / len(pieces), high / len(pieces))
        return jnp.repeat(jnp.exp(heights), dims[dim] // blocks).reshape((-1,) + (1,) * (len(dims) - dim - 1))

    loudness = one(*pieces[0])
    for cut in pieces[1:]:
        loudness = loudness * one(*cut)
    return loudness


def routed_block(key, own, number, rows, number_of, top, bound, slope):
    order = jax.random.permutation(key, number_of)
    packed, usual = shares(number_of, rows * top, bound, slope, True), shares(number_of, rows * top, bound, slope, False)
    places = jnp.arange(number_of)

    def named(sizes, turn):
        used = int((sizes > 0).sum())
        fixed = max(1, used // 4)
        passed = fixed + (places - fixed + turn * (used - fixed)) % max(1, number_of - fixed)
        return jnp.zeros((number_of,), jnp.int32).at[order[jnp.where(places < fixed, places, passed)]].set(jnp.asarray(sizes, jnp.int32))

    sizes = jnp.where(number % 4 == 0, named(packed, number // 4), named(usual, number - number // 4 - 1))
    mixed = jax.random.permutation(jax.random.fold_in(own, 3), number_of)
    giver, receiver = mixed[0:number_of // 2 * 2:2], mixed[1:number_of // 2 * 2:2]
    margin = jnp.minimum(sizes[giver] - 1, bound - sizes[receiver]) // 2
    margin = jnp.where((giver == order[0]) | (receiver == order[0]) | (sizes[receiver] == 0), 0, jnp.maximum(margin, 0))
    passed = jax.random.randint(jax.random.fold_in(own, 4), (number_of // 2,), 0, 1 << 20) % (margin + 1)
    sizes = sizes.at[giver].add(-passed).at[receiver].add(passed)
    labels = jnp.searchsorted(jnp.cumsum(sizes), jnp.arange(rows * top), side="right").astype(jnp.int32)
    listing = labels.reshape(top, rows).T
    listing = listing[jax.random.permutation(jax.random.fold_in(own, 1), rows)]
    turn = jax.random.randint(jax.random.fold_in(own, 2), (rows, 1), 0, top)
    return jnp.take_along_axis(listing, (jnp.arange(top)[None, :] + turn) % top, axis=1)


def shares(count, total, limit, slope, full):
    loads = [(1 << 20) // math.isqrt(rank ** slope) + 1 for rank in range(1, count + 1)]
    largest = limit if full else min(limit, max(-(-total // count), total * loads[0] // sum(loads)))
    least = 1 if total - largest >= count - 1 else 0
    holding, spare = [largest] + [least] * (count - 1), total - largest - least * (count - 1)
    while spare > 0:
        candidates = [i for i in range(1, count) if holding[i] < largest] or [i for i in range(1, count) if holding[i] < limit]
        pool, left = sum([loads[i] for i in candidates]), spare
        for i in candidates:
            extra = min(limit - holding[i], max(1, left * loads[i] // pool), spare)
            holding[i] = holding[i] + extra
            spare = spare - extra
    return np.array(holding)


def scatter_about(rng, dims, scale, reach, cuts=(), held_as=jnp.bfloat16):
    result = jax.random.normal(rng, dims, jnp.float32) * scale
    if len(cuts) > 0:
        result = level_of(rng, dims, cuts, -0.22, 0.18) * result
    return jnp.clip(result, min=-reach, max=reach).astype(held_as)


def setup_inputs(seed: int = 0) -> dict:
    key_list = jax.random.split(jax.random.key(seed), 8)
    inputs = scatter_about(key_list[0], (TOKENS, D), 1.0, 6.0, ((0, 256),))
    out_grad = scatter_about(key_list[1], (TOKENS, D), 0.5, 3.0, ((0, 256),))
    expert_ids_keys = jax.random.split(jax.random.fold_in(key_list[2], 1), TOKENS // TOK_DEV)
    expert_ids_turns = jax.random.permutation(jax.random.fold_in(key_list[2], 3), TOKENS // TOK_DEV)
    expert_ids = jax.vmap(lambda own, number: routed_block(jax.random.fold_in(key_list[2], 2), own, number, TOK_DEV, EXPERTS, TOPK, CAP, 2))(expert_ids_keys, expert_ids_turns).reshape((TOKENS, TOPK))
    gates = jnp.clip(0.1 + 0.9 * jax.random.uniform(key_list[3], (TOKENS, TOPK), jnp.float32) ** level_of(key_list[3], (TOKENS, TOPK), ((0, 256),), -0.2, 0.2), 0.1, 1.0)
    gate_w = scatter_about(key_list[4], (EXPERTS, D, H), D ** -0.5, 0.125, ((0, 128), (1, 2)))
    up_w = scatter_about(key_list[5], (EXPERTS, D, H), D ** -0.5, 0.125, ((0, 128), (1, 2)))
    down_w = scatter_about(key_list[6], (EXPERTS, H, D), H ** -0.5, 0.21875, ((0, 128), (2, 2)))
    return {"inputs": inputs, "out_grad": out_grad, "expert_ids": expert_ids, "gates": gates, "gate_w": gate_w, "up_w": up_w, "down_w": down_w}


def reference(inputs, out_grad, expert_ids, gates, gate_w, up_w, down_w):
    block_count = TOKENS // TOK_DEV
    pair_count = TOK_DEV * TOPK
    slot_rows = GROUPS * CAP
    block_ids = expert_ids.reshape(block_count, pair_count).astype(jnp.int32)
    one_hot = (block_ids[:, :, None] == jnp.arange(EXPERTS, dtype=jnp.int32)[None, None, :]).astype(jnp.int32)
    rank_index = jnp.sum(jnp.cumsum(one_hot, axis=1, dtype=jnp.int32) * one_hot, axis=2, dtype=jnp.int32) - 1
    block_index = jnp.arange(block_count, dtype=jnp.int32)[:, None]
    replica = jnp.broadcast_to(block_index % REPLICAS, (block_count, pair_count)).astype(jnp.int32)
    position = ((block_index // REPLICAS) * CAP + rank_index).astype(jnp.int32)
    pair_index = jnp.arange(block_count * pair_count, dtype=jnp.int32).reshape(block_count, pair_count)
    sentinel = block_count * pair_count
    table = jnp.full((REPLICAS, EXPERTS, slot_rows), sentinel, jnp.int32)
    table = table.at[replica, block_ids, position].set(pair_index)
    token_of = jnp.where(table == sentinel, TOKENS, table // TOPK).astype(jnp.int32)
    input_pad = jnp.concatenate([inputs, jnp.zeros((1, D), inputs.dtype)], axis=0)
    grad_pad = jnp.concatenate([out_grad, jnp.zeros((1, D), out_grad.dtype)], axis=0)
    gate_pad = jnp.concatenate([gates.reshape(-1), jnp.zeros((1,), gates.dtype)], axis=0)
    gate_rows = gate_pad[table]
    token_by_expert = jnp.transpose(token_of, (1, 0, 2))
    gate_by_expert = jnp.transpose(gate_rows, (1, 0, 2))

    def per_expert(operands):
        token_rows, gate_col, w_gate, w_up, w_down = operands
        rows_in = input_pad[token_rows]
        scaled = (gate_col[:, :, None].astype(jnp.float32) * grad_pad[token_rows].astype(jnp.float32)).astype(jnp.bfloat16)
        rows_f = rows_in.astype(jnp.float32)
        scaled_f = scaled.astype(jnp.float32)
        gate_f = w_gate.astype(jnp.float32)
        up_f = w_up.astype(jnp.float32)
        down_f = w_down.astype(jnp.float32)
        gate_act = jnp.einsum('rsd,dh->rsh', rows_f, gate_f)
        up_act = jnp.einsum('rsd,dh->rsh', rows_f, up_f)
        sigma = jax.nn.sigmoid(gate_act)
        silu_val = gate_act * sigma
        hidden = (silu_val * up_act).astype(jnp.bfloat16)
        hidden_grad = jnp.einsum('rsd,hd->rsh', scaled_f, down_f)
        gate_grad = (hidden_grad * up_act * sigma * (1.0 + gate_act * (1.0 - sigma))).astype(jnp.bfloat16)
        up_grad = (hidden_grad * silu_val).astype(jnp.bfloat16)
        gate_grad_f = gate_grad.astype(jnp.float32)
        up_grad_f = up_grad.astype(jnp.float32)
        slot_grad = (jnp.einsum('rsh,dh->rsd', gate_grad_f, gate_f) + jnp.einsum('rsh,dh->rsd', up_grad_f, up_f)).astype(jnp.bfloat16)
        gate_part = jnp.einsum('rsd,rsh->rdh', rows_f, gate_grad_f).astype(jnp.bfloat16)
        up_part = jnp.einsum('rsd,rsh->rdh', rows_f, up_grad_f).astype(jnp.bfloat16)
        down_part = jnp.einsum('rsh,rsd->rhd', hidden.astype(jnp.float32), scaled_f).astype(jnp.bfloat16)
        gate_part, up_part, down_part = lax.optimization_barrier((gate_part, up_part, down_part))
        gate_sum = jnp.sum(gate_part.astype(jnp.float32), axis=0).astype(jnp.bfloat16)
        up_sum = jnp.sum(up_part.astype(jnp.float32), axis=0).astype(jnp.bfloat16)
        down_sum = jnp.sum(down_part.astype(jnp.float32), axis=0).astype(jnp.bfloat16)
        return slot_grad, gate_sum, up_sum, down_sum

    slot_grads, gate_w_grad, up_w_grad, down_w_grad = lax.map(
        per_expert, (token_by_expert, gate_by_expert, gate_w, up_w, down_w))
    picked = slot_grads[block_ids, replica, position]
    input_grad = jnp.sum(picked.reshape(TOKENS, TOPK, D).astype(jnp.float32), axis=1).astype(jnp.bfloat16)
    return input_grad, gate_w_grad, up_w_grad, down_w_grad
```

```python
import functools

import jax
import jax.numpy as jnp
from jax import lax
from jax.experimental import pallas as pl
from jax.experimental.pallas import tpu as pltpu
from jax.sharding import PartitionSpec as P

RING = 8
CAP = 4
META = 128
HALF = 1024
COLS = 1024
HTILE = 256
WTILE = 256
CHUNKS = ((0,), (1, -1), (2, -2), (3, -3, 4))
BF = jnp.bfloat16
F32 = jnp.float32
VMEM_LIMIT = 32 * 1024 * 1024
TOKEN_COST = pl.CostEstimate(flops=1, bytes_accessed=1, transcendentals=0)


def far_memory(values):
    return [pltpu.with_memory_space_constraint(value, pltpu.HBM) for value in values]


def dot(a, b, ca, cb):
    return lax.dot_general(a, b, (((ca,), (cb,)), ((), ())), preferred_element_type=F32)


def by_token(columns):
    tokens = columns.shape[0]
    same = lax.broadcasted_iota(jnp.int32, (tokens, tokens), 0) == lax.broadcasted_iota(
        jnp.int32, (tokens, tokens), 1
    )
    return dot(columns, same.astype(F32).astype(BF), 0, 0)


def hits(meta, owner, slot):
    tokens = meta.shape[1]
    first = owner == meta[0:1, :].astype(jnp.int32)
    second = owner == meta[1:2, :].astype(jnp.int32)
    named = (first | second).astype(F32).astype(BF)
    before = (
        lax.broadcasted_iota(jnp.int32, (tokens, tokens), 0)
        < lax.broadcasted_iota(jnp.int32, (tokens, tokens), 1)
    )
    rank = dot(named, before.astype(F32).astype(BF), 1, 0)
    hit = (first | second) & (rank.astype(jnp.int32) == slot)
    gate_first = meta[2:3, :] + meta[3:4, :] + meta[4:5, :]
    gate_second = meta[5:6, :] + meta[6:7, :] + meta[7:8, :]
    gate = jnp.where(first, gate_first, 0.0) + jnp.where(second, gate_second, 0.0)
    return hit, jnp.sum(jnp.where(hit, gate, 0.0), axis=1, keepdims=True)


def pack_kernel(x_ref, grad_ref, ids_ref, gates_ref, out_ref):
    width = x_ref.shape[1]
    tokens = x_ref.shape[0]
    out_ref[:, 0:width] = x_ref[...]
    out_ref[:, width : 2 * width] = grad_ref[...]
    lane = lax.broadcasted_iota(jnp.int32, (tokens, META), 1)
    packed = jnp.zeros((tokens, META), F32)
    for k in range(2):
        packed = jnp.where(lane == k, ids_ref[:, k : k + 1].astype(F32), packed)
        rest = gates_ref[:, k : k + 1]
        for part in range(3):
            piece = rest.astype(BF).astype(F32)
            packed = jnp.where(lane == 2 + 3 * k + part, piece, packed)
            rest = rest - piece
    out_ref[:, 2 * width :] = packed.astype(BF)


def pack(x, grad, ids, gates):
    return pl.pallas_call(
        pack_kernel,
        out_shape=jax.ShapeDtypeStruct((x.shape[0], 2 * x.shape[1] + META), BF),
        compiler_params=pltpu.CompilerParams(vmem_limit_bytes=VMEM_LIMIT),
        cost_estimate=TOKEN_COST,
    )(*far_memory([x, grad]), ids, gates)


def build_kernel(jobs, sources, outs, waits, place_ref, *refs):
    refs = refs[waits:]
    metas, data = refs[:sources], refs[sources : 3 * sources]
    out_refs, picks = refs[3 * sources : 3 * sources + outs], refs[3 * sources + outs :]
    place = place_ref[0]

    @pl.when(pl.program_id(0) == 0)
    def _():
        by = [by_token(meta[...]) for meta in metas]
        for number, (source, offset, start, groups, _, _, _) in enumerate(jobs):
            pick, scale = picks[2 * number], picks[2 * number + 1]
            row = lax.broadcasted_iota(jnp.int32, (groups * 2 * CAP, 128), 0)
            owner = ((row >> 3) + start) * RING + lax.rem(place + offset + RING, RING)
            is_grad = ((row >> 2) & 1) == 1
            hit, gate = hits(by[source], owner, row & 3)
            pick[:, 0:128] = (hit & ~is_grad).astype(F32).astype(BF)
            pick[:, 128:256] = (hit & is_grad).astype(F32).astype(BF)
            scale[...] = jnp.where(is_grad, gate, 1.0)

    for number, (source, _, _, groups, out, to, at) in enumerate(jobs):
        stacked = jnp.concatenate([data[2 * source][...], data[2 * source + 1][...]], axis=0)
        value = dot(picks[2 * number][...], stacked, 1, 0) * picks[2 * number + 1][:, 0:1]
        out_refs[out][to : to + groups, at] = value.astype(BF).reshape(
            groups, 2 * CAP, value.shape[1]
        )


def build(jobs, place, planes, shapes, after=()):
    features = (planes[0].shape[1] - META) // 2
    sources = len(planes)
    tokens = planes[0].shape[0]
    steps = features // COLS
    scratch = []
    for job in jobs:
        rows = job[3] * 2 * CAP
        scratch += [pltpu.VMEM((rows, 256), BF), pltpu.VMEM((rows, 128), F32)]
    shapes = [shape + (2 * CAP,) for shape in shapes]
    return pl.pallas_call(
        functools.partial(build_kernel, jobs, sources, len(shapes), len(after)),
        grid=(steps,),
        out_shape=[pltpu.HBM(shape + (features,), BF) for shape in shapes],
        in_specs=[pl.BlockSpec(memory_space=pltpu.SMEM)]
        + [pl.BlockSpec(memory_space=pl.ANY) for _ in after]
        + [pl.BlockSpec((tokens, META), lambda c: (0, 2 * features // META))] * sources
        + [
            pl.BlockSpec((tokens, COLS), lambda c: (0, c)),
            pl.BlockSpec((tokens, COLS), lambda c: (0, c + steps)),
        ]
        * sources,
        out_specs=[pl.BlockSpec(shape + (COLS,), lambda c: (0, 0, 0, c)) for shape in shapes],
        scratch_shapes=scratch,
        compiler_params=pltpu.CompilerParams(vmem_limit_bytes=VMEM_LIMIT),
        cost_estimate=TOKEN_COST,
    )(place, *after, *planes, *[p for p in planes for _ in range(2)])


def join_kernel(left_ref, right_ref, far_left_ref, far_right_ref, after_ref, out_ref):
    del after_ref
    half = far_left_ref.shape[0]
    out_ref[:, 0:1] = left_ref[...]
    out_ref[:, 1:2] = right_ref[...]
    out_ref[0:half, 2:3] = far_left_ref[...]
    out_ref[half:, 2:3] = far_right_ref[...]


def join(third, fourth, groups, after):
    features = third[0].shape[3]
    shape = (groups, 1, 2 * CAP)
    specs = [pl.BlockSpec(shape + (COLS,), lambda c: (0, 0, 0, c))] * 2
    specs += [pl.BlockSpec(v.shape[:3] + (COLS,), lambda c: (0, 0, 0, c)) for v in fourth]
    return pl.pallas_call(
        join_kernel,
        grid=(features // COLS,),
        out_shape=pltpu.HBM((groups, 3, 2 * CAP, features), BF),
        in_specs=specs + [pl.BlockSpec(memory_space=pl.ANY)],
        out_specs=pl.BlockSpec((groups, 3, 2 * CAP, COLS), lambda c: (0, 0, 0, c)),
        compiler_params=pltpu.CompilerParams(vmem_limit_bytes=VMEM_LIMIT),
        cost_estimate=TOKEN_COST,
    )(*third, *fourth, after)


def expert_kernel(chunks, groups, place_ref, *refs):
    recvs, refs = refs[: len(chunks)], refs[len(chunks) :]
    wg_own, wg_oth, wu_own, wu_oth, wd_own, wd_oth = refs[:6]
    x_own, x_oth, s_own, s_oth, hid_ref, gg_ref, ug_ref, back = refs[6:14]
    acc_own, acc_oth, stage, sems = refs[14:]
    step = pl.program_id(0)
    place = place_ref[0]
    rep = place_ref[1]

    @pl.when(step == 0)
    def _():
        start = 0
        for recv, planes in zip(recvs, chunks):
            slots = groups * len(planes) * CAP
            row = lax.broadcasted_iota(jnp.int32, (slots, 2 * slots), 0)
            col = lax.broadcasted_iota(jnp.int32, (slots, 2 * slots), 1)
            source = (row >> 2) * 8 + (row & 3)
            take_x = (col == source).astype(F32).astype(BF)
            take_s = (col == source + 4).astype(F32).astype(BF)
            for half, x_ref, s_ref in ((rep, x_own, s_own), (1 - rep, x_oth, s_oth)):
                at = pl.ds(pl.multiple_of(half * HALF, HALF), HALF)
                rows = recv[:, :, :, at].reshape(2 * slots, HALF)
                x_ref[start : start + slots] = dot(take_x, rows, 1, 0).astype(BF)
                s_ref[start : start + slots] = dot(take_s, rows, 1, 0).astype(BF)
            start += slots

    gate = dot(x_own[...], wg_own[...], 1, 0) + dot(x_oth[...], wg_oth[...], 1, 0)
    up = dot(x_own[...], wu_own[...], 1, 0) + dot(x_oth[...], wu_oth[...], 1, 0)
    hidden_grad = dot(s_own[...], wd_own[...], 1, 1) + dot(s_oth[...], wd_oth[...], 1, 1)
    sigma = jax.nn.sigmoid(gate)
    silu = gate * sigma
    hid_ref[...] = (silu * up).astype(BF)
    gate_grad = (hidden_grad * up * sigma * (1.0 + gate * (1.0 - sigma))).astype(BF)
    up_grad = (hidden_grad * silu).astype(BF)
    gg_ref[...] = gate_grad
    ug_ref[...] = up_grad
    new_own = dot(gate_grad, wg_own[...], 1, 1) + dot(up_grad, wu_own[...], 1, 1)
    new_oth = dot(gate_grad, wg_oth[...], 1, 1) + dot(up_grad, wu_oth[...], 1, 1)

    @pl.when(step == 0)
    def _():
        acc_own[...] = new_own
        acc_oth[...] = new_oth

    @pl.when(step > 0)
    def _():
        acc_own[...] += new_own
        acc_oth[...] += new_oth

    @pl.when(step == pl.num_programs(0) - 1)
    def _():
        start = 0
        first = 0
        copies = []
        for planes in chunks:
            count = len(planes)
            slots = groups * count * CAP
            row = lax.broadcasted_iota(jnp.int32, (2 * slots, slots), 0)
            col = lax.broadcasted_iota(jnp.int32, (2 * slots, slots), 1)
            same = ((row >> 3) == (col >> 2)) & ((row & 3) == (col & 3))
            upper = (row >> 2) & 1
            put_own = (same & (upper == rep)).astype(F32).astype(BF)
            put_oth = (same & (upper != rep)).astype(F32).astype(BF)
            mixed = dot(put_own, acc_own[start : start + slots].astype(BF), 1, 0) + dot(
                put_oth, acc_oth[start : start + slots].astype(BF), 1, 0
            )
            stage[:, first : first + count] = mixed.astype(BF).reshape(
                groups, count, 2 * CAP, HALF
            )
            for index, plane in enumerate(planes):
                copy = pltpu.make_async_copy(
                    stage.at[:, first + index],
                    back.at[:, lax.rem(place - plane + RING, RING)],
                    sems.at[first + index],
                )
                copy.start()
                copies.append(copy)
            start += slots
            first += count
        for copy in copies:
            copy.wait()


def experts(chunks, groups, place, recvs, weights):
    slots = groups * RING * CAP
    hidden = weights[0].shape[1]
    wide = pl.BlockSpec((HALF, HTILE), lambda h: (0, h))
    tall = pl.BlockSpec((HTILE, HALF), lambda h: (h, 0))
    rows = pl.BlockSpec((slots, HALF), lambda h: (0, 0))
    tile = pl.BlockSpec((slots, HTILE), lambda h: (0, h))
    return pl.pallas_call(
        functools.partial(expert_kernel, chunks, groups),
        grid=(hidden // HTILE,),
        out_shape=(
            [pltpu.HBM((slots, HALF), BF)] * 4
            + [pltpu.HBM((slots, hidden), BF)] * 3
            + [pltpu.HBM((groups, RING, 2 * CAP, HALF), BF)]
        ),
        in_specs=[pl.BlockSpec(memory_space=pltpu.SMEM)]
        + [
            pl.BlockSpec(r.shape, lambda h: (0, 0, 0, 0), pipeline_mode=pl.Buffered(1))
            for r in recvs
        ]
        + [wide] * 4
        + [tall] * 2,
        out_specs=[rows] * 4 + [tile] * 3 + [pl.BlockSpec(memory_space=pl.ANY)],
        scratch_shapes=[
            pltpu.VMEM((slots, HALF), F32),
            pltpu.VMEM((slots, HALF), F32),
            pltpu.VMEM((groups, RING, 2 * CAP, HALF), BF),
            pltpu.SemaphoreType.DMA((RING,)),
        ],
        compiler_params=pltpu.CompilerParams(vmem_limit_bytes=48 * 1024 * 1024),
        cost_estimate=TOKEN_COST,
    )(place, *far_memory(recvs[:3]), recvs[3], *far_memory(weights))


def weight_kernel(has_sum, x_ref, s_ref, gate_ref, up_ref, hid_ref, *refs):
    outs = refs[-3:]
    parts = (
        dot(x_ref[...], gate_ref[...], 0, 0),
        dot(x_ref[...], up_ref[...], 0, 0),
        dot(hid_ref[...], s_ref[...], 0, 0),
    )
    for index, part in enumerate(parts):
        part = part.astype(BF)
        if has_sum:
            part = (part.astype(F32) + refs[index][...].astype(F32)).astype(BF)
        outs[index][...] = part


def weight_grads(x, s, gate, up, hid, received):
    slots, hidden = gate.shape
    wide = pl.BlockSpec((WTILE, hidden), lambda c: (c, 0))
    tall = pl.BlockSpec((hidden, WTILE), lambda c: (0, c))
    part_specs = [wide, wide, tall]
    return pl.pallas_call(
        functools.partial(weight_kernel, bool(received)),
        grid=(HALF // WTILE,),
        out_shape=[
            pltpu.HBM((HALF, hidden), BF),
            pltpu.HBM((HALF, hidden), BF),
            pltpu.HBM((hidden, HALF), BF),
        ],
        in_specs=[pl.BlockSpec((slots, WTILE), lambda c: (0, c))] * 2
        + [pl.BlockSpec((slots, hidden), lambda c: (0, 0))] * 3
        + (part_specs if received else []),
        out_specs=part_specs,
        compiler_params=pltpu.CompilerParams(vmem_limit_bytes=VMEM_LIMIT),
        cost_estimate=TOKEN_COST,
    )(*far_memory([x, s, gate, up, hid]), *received)


def combine_kernel(meta_ref, back_ref, out_ref):
    rows = back_ref.shape[0]
    row = lax.broadcasted_iota(jnp.int32, (rows, 128), 0)
    hit, _ = hits(by_token(meta_ref[...]), row >> 3, row & 3)
    upper = ((row >> 2) & 1) == 1
    low = (hit & ~upper).astype(F32).astype(BF)
    high = (hit & upper).astype(F32).astype(BF)
    out_ref[:, 0:HALF] = dot(low, back_ref[...], 0, 0).astype(BF)
    out_ref[:, HALF : 2 * HALF] = dot(high, back_ref[...], 0, 0).astype(BF)


def combine(packed, back):
    rows = back.shape[0]
    return pl.pallas_call(
        combine_kernel,
        grid=(1,),
        out_shape=jax.ShapeDtypeStruct((128, 2 * HALF), BF),
        in_specs=[
            pl.BlockSpec((128, META), lambda c: (0, 4 * HALF // META)),
            pl.BlockSpec((rows, HALF), lambda c: (0, 0)),
        ],
        out_specs=pl.BlockSpec((128, 2 * HALF), lambda c: (0, 0)),
        compiler_params=pltpu.CompilerParams(vmem_limit_bytes=VMEM_LIMIT),
        cost_estimate=TOKEN_COST,
    )(packed, back)


def local(inputs, out_grad, expert_ids, gates, gate_w, up_w, down_w):
    owners = lax.axis_size("expert")
    groups = owners // RING
    across = [[g * RING + z for g in range(groups)] for z in range(RING)]
    place = jnp.stack(
        [lax.rem(lax.axis_index("expert"), RING), lax.axis_index("rep")]
    ).astype(jnp.int32)

    def hop(value, by):
        pairs = [(g * RING + z, g * RING + (z + by) % RING) for g in range(groups) for z in range(RING)]
        return lax.ppermute(value, "expert", pairs)

    def swap(value):
        return lax.ppermute(value, "rep", [(0, 1), (1, 0)])

    packed = pack(inputs, out_grad, expert_ids, gates)
    data = {0: packed, 1: hop(packed, 1), -1: hop(packed, -1)}
    own = (gate_w[0], up_w[0], down_w[0])
    oth = tuple(swap(w) for w in own)
    weights = (own[0], oth[0], own[1], oth[1], own[2], oth[2])

    def near(planes, after):
        jobs = tuple((i, 0, 0, groups, 0, 0, i) for i in range(len(planes)))
        (sent,) = build(
            jobs,
            place,
            [data[p] for p in planes],
            [(groups, len(planes))],
            after,
        )
        return sent

    def exchange(sent):
        return lax.all_to_all(
            sent, "expert", split_axis=0, concat_axis=0, tiled=True, axis_index_groups=across
        )

    recv_own = exchange(near(CHUNKS[0], ()))
    recv_own, data[1], data[-1] = lax.optimization_barrier((recv_own, data[1], data[-1]))
    for by in (1, -1):
        data[2 * by] = hop(data[by], by)
    recv_next = exchange(near(CHUNKS[1], ()))
    half = groups // 2
    far = build(
        (
            (0, 1, 0, groups, 0, 0, 0),
            (0, 2, 0, half, 0, groups, 0),
            (1, -1, 0, groups, 1, 0, 0),
            (1, -2, half, groups - half, 1, groups, 0),
        ),
        place,
        [data[2], data[-2]],
        [(groups + half, 1), (2 * groups - half, 1)],
        (),
    )
    third = (hop(far[0], 1), hop(far[1], -1))
    recv_second = exchange(near(CHUNKS[2], far_memory([far[0], recv_next])))
    fourth = (hop(third[0][groups:], 1), hop(third[1][groups:], -1))
    recv_far = exchange(join(third, fourth, groups, recv_second))
    x_own, x_oth, s_own, s_oth, hid, gate_grad, up_grad, back = experts(
        CHUNKS, groups, place, (recv_own, recv_next, recv_second, recv_far), weights
    )
    returned = lax.all_to_all(
        back.reshape(owners, 2 * CAP, HALF), "expert", split_axis=0, concat_axis=0, tiled=True
    )
    theirs = weight_grads(x_oth, s_oth, gate_grad, up_grad, hid, ())
    received = tuple(swap(part) for part in theirs)
    grads = weight_grads(x_own, s_own, gate_grad, up_grad, hid, received)
    input_grad = combine(packed, returned.reshape(owners * 2 * CAP, HALF))
    return (input_grad, grads[0][None], grads[1][None], grads[2][None])


def solution(mesh):
    return jax.shard_map(
        local,
        mesh=mesh,
        in_specs=(
            P(("expert", "rep"), None),
            P(("expert", "rep"), None),
            P(("expert", "rep"), None),
            P(("expert", "rep"), None),
            P("expert", "rep", None),
            P("expert", "rep", None),
            P("expert", None, "rep"),
        ),
        out_specs=(
            P(("expert", "rep"), None),
            P("expert", "rep", None),
            P("expert", "rep", None),
            P("expert", None, "rep"),
        ),
        check_vma=False,
    )
```

```python
import functools

import jax
import jax.numpy as jnp
from jax import lax
from jax.experimental import pallas as pl
from jax.experimental.pallas import tpu as pltpu
from jax.sharding import PartitionSpec as P

RING = 8
CAP = 4
META = 128
EXPERT_LIMIT = 40 * 1024 * 1024
HALF = 1024
COLS = 1024
HTILE = 256
WTILE = 256
CHUNKS = ((0,), (1, -1), (2, -2), (3, -3, 4))
BF = jnp.bfloat16
F32 = jnp.float32
VMEM_LIMIT = 32 * 1024 * 1024
TOKEN_COST = pl.CostEstimate(flops=1, bytes_accessed=1, transcendentals=0)


def far_memory(values):
    return [pltpu.with_memory_space_constraint(value, pltpu.HBM) for value in values]


def dot(a, b, ca, cb):
    return lax.dot_general(a, b, (((ca,), (cb,)), ((), ())), preferred_element_type=F32)


def by_token(columns):
    tokens = columns.shape[0]
    same = lax.broadcasted_iota(jnp.int32, (tokens, tokens), 0) == lax.broadcasted_iota(
        jnp.int32, (tokens, tokens), 1
    )
    return dot(columns, same.astype(F32).astype(BF), 0, 0)


def hits(meta, owner, slot):
    tokens = meta.shape[1]
    first = owner == meta[0:1, :].astype(jnp.int32)
    second = owner == meta[1:2, :].astype(jnp.int32)
    named = (first | second).astype(F32).astype(BF)
    before = (
        lax.broadcasted_iota(jnp.int32, (tokens, tokens), 0)
        < lax.broadcasted_iota(jnp.int32, (tokens, tokens), 1)
    )
    rank = dot(named, before.astype(F32).astype(BF), 1, 0)
    hit = (first | second) & (rank.astype(jnp.int32) == slot)
    gate_first = meta[2:3, :] + meta[3:4, :] + meta[4:5, :]
    gate_second = meta[5:6, :] + meta[6:7, :] + meta[7:8, :]
    gate = jnp.where(first, gate_first, 0.0) + jnp.where(second, gate_second, 0.0)
    return hit, jnp.sum(jnp.where(hit, gate, 0.0), axis=1, keepdims=True)


def pack_kernel(x_ref, grad_ref, ids_ref, gates_ref, out_ref):
    width = x_ref.shape[1]
    tokens = x_ref.shape[0]
    out_ref[:, 0:width] = x_ref[...]
    out_ref[:, width : 2 * width] = grad_ref[...]
    lane = lax.broadcasted_iota(jnp.int32, (tokens, META), 1)
    packed = jnp.zeros((tokens, META), F32)
    for k in range(2):
        packed = jnp.where(lane == k, ids_ref[:, k : k + 1].astype(F32), packed)
        rest = gates_ref[:, k : k + 1]
        for part in range(3):
            piece = rest.astype(BF).astype(F32)
            packed = jnp.where(lane == 2 + 3 * k + part, piece, packed)
            rest = rest - piece
    out_ref[:, 2 * width :] = packed.astype(BF)


def pack(x, grad, ids, gates):
    return pl.pallas_call(
        pack_kernel,
        out_shape=jax.ShapeDtypeStruct((x.shape[0], 2 * x.shape[1] + META), BF),
        compiler_params=pltpu.CompilerParams(vmem_limit_bytes=VMEM_LIMIT),
        cost_estimate=TOKEN_COST,
    )(*far_memory([x, grad]), ids, gates)


def build_kernel(jobs, sources, outs, waits, place_ref, *refs):
    refs = refs[waits:]
    metas, data = refs[:sources], refs[sources : 3 * sources]
    out_refs, picks = refs[3 * sources : 3 * sources + outs], refs[3 * sources + outs :]
    place = place_ref[0]

    @pl.when(pl.program_id(0) == 0)
    def _():
        by = [by_token(meta[...]) for meta in metas]
        for number, (source, offset, start, groups, _, _, _) in enumerate(jobs):
            pick, scale = picks[2 * number], picks[2 * number + 1]
            row = lax.broadcasted_iota(jnp.int32, (groups * 2 * CAP, 128), 0)
            owner = ((row >> 3) + start) * RING + lax.rem(place + offset + RING, RING)
            is_grad = ((row >> 2) & 1) == 1
            hit, gate = hits(by[source], owner, row & 3)
            pick[:, 0:128] = (hit & ~is_grad).astype(F32).astype(BF)
            pick[:, 128:256] = (hit & is_grad).astype(F32).astype(BF)
            scale[...] = jnp.where(is_grad, gate, 1.0)

    for number, (source, _, _, groups, out, to, at) in enumerate(jobs):
        stacked = jnp.concatenate([data[2 * source][...], data[2 * source + 1][...]], axis=0)
        value = dot(picks[2 * number][...], stacked, 1, 0) * picks[2 * number + 1][:, 0:1]
        out_refs[out][to : to + groups, at] = value.astype(BF).reshape(
            groups, 2 * CAP, value.shape[1]
        )


def build(jobs, place, planes, shapes, after=()):
    features = (planes[0].shape[1] - META) // 2
    sources = len(planes)
    tokens = planes[0].shape[0]
    steps = features // COLS
    scratch = []
    for job in jobs:
        rows = job[3] * 2 * CAP
        scratch += [pltpu.VMEM((rows, 256), BF), pltpu.VMEM((rows, 128), F32)]
    shapes = [shape + (2 * CAP,) for shape in shapes]
    return pl.pallas_call(
        functools.partial(build_kernel, jobs, sources, len(shapes), len(after)),
        grid=(steps,),
        out_shape=[pltpu.HBM(shape + (features,), BF) for shape in shapes],
        in_specs=[pl.BlockSpec(memory_space=pltpu.SMEM)]
        + [pl.BlockSpec(memory_space=pl.ANY) for _ in after]
        + [pl.BlockSpec((tokens, META), lambda c: (0, 2 * features // META))] * sources
        + [
            pl.BlockSpec((tokens, COLS), lambda c: (0, c)),
            pl.BlockSpec((tokens, COLS), lambda c: (0, c + steps)),
        ]
        * sources,
        out_specs=[pl.BlockSpec(shape + (COLS,), lambda c: (0, 0, 0, c)) for shape in shapes],
        scratch_shapes=scratch,
        compiler_params=pltpu.CompilerParams(vmem_limit_bytes=VMEM_LIMIT),
        cost_estimate=TOKEN_COST,
    )(place, *after, *planes, *[p for p in planes for _ in range(2)])


def join_kernel(left_ref, right_ref, far_left_ref, far_right_ref, after_ref, out_ref):
    del after_ref
    half = far_left_ref.shape[0]
    out_ref[:, 0:1] = left_ref[...]
    out_ref[:, 1:2] = right_ref[...]
    out_ref[0:half, 2:3] = far_left_ref[...]
    out_ref[half:, 2:3] = far_right_ref[...]


def join(third, fourth, groups, after):
    features = third[0].shape[3]
    shape = (groups, 1, 2 * CAP)
    specs = [pl.BlockSpec(shape + (COLS,), lambda c: (0, 0, 0, c))] * 2
    specs += [pl.BlockSpec(v.shape[:3] + (COLS,), lambda c: (0, 0, 0, c)) for v in fourth]
    return pl.pallas_call(
        join_kernel,
        grid=(features // COLS,),
        out_shape=pltpu.HBM((groups, 3, 2 * CAP, features), BF),
        in_specs=specs + [pl.BlockSpec(memory_space=pl.ANY)],
        out_specs=pl.BlockSpec((groups, 3, 2 * CAP, COLS), lambda c: (0, 0, 0, c)),
        compiler_params=pltpu.CompilerParams(vmem_limit_bytes=VMEM_LIMIT),
        cost_estimate=TOKEN_COST,
    )(*third, *fourth, after)


def expert_kernel(chunks, groups, has_base, place_ref, *refs):
    refs = refs[1:] if has_base else refs
    recvs, refs = refs[: len(chunks)], refs[len(chunks) :]
    wg_own, wg_oth, wu_own, wu_oth, wd_own, wd_oth = refs[:6]
    x_own, x_oth, s_own, s_oth, hid_ref, gg_ref, ug_ref, back = refs[6:14]
    acc_own, acc_oth, stage, sems = refs[14:]
    step = pl.program_id(0)
    place = place_ref[0]
    rep = place_ref[1]

    @pl.when(step == 0)
    def _():
        start = 0
        for recv, planes in zip(recvs, chunks):
            slots = groups * len(planes) * CAP
            row = lax.broadcasted_iota(jnp.int32, (slots, 2 * slots), 0)
            col = lax.broadcasted_iota(jnp.int32, (slots, 2 * slots), 1)
            source = (row >> 2) * 8 + (row & 3)
            take_x = (col == source).astype(F32).astype(BF)
            take_s = (col == source + 4).astype(F32).astype(BF)
            for half, x_ref, s_ref in ((rep, x_own, s_own), (1 - rep, x_oth, s_oth)):
                at = pl.ds(pl.multiple_of(half * HALF, HALF), HALF)
                rows = recv[:, :, :, at].reshape(2 * slots, HALF)
                x_ref[start : start + slots] = dot(take_x, rows, 1, 0).astype(BF)
                s_ref[start : start + slots] = dot(take_s, rows, 1, 0).astype(BF)
            start += slots

    gate = dot(x_own[...], wg_own[...], 1, 0) + dot(x_oth[...], wg_oth[...], 1, 0)
    up = dot(x_own[...], wu_own[...], 1, 0) + dot(x_oth[...], wu_oth[...], 1, 0)
    hidden_grad = dot(s_own[...], wd_own[...], 1, 1) + dot(s_oth[...], wd_oth[...], 1, 1)
    sigma = jax.nn.sigmoid(gate)
    silu = gate * sigma
    hid_ref[...] = (silu * up).astype(BF)
    gate_grad = (hidden_grad * up * sigma * (1.0 + gate * (1.0 - sigma))).astype(BF)
    up_grad = (hidden_grad * silu).astype(BF)
    gg_ref[...] = gate_grad
    ug_ref[...] = up_grad
    new_own = dot(gate_grad, wg_own[...], 1, 1) + dot(up_grad, wu_own[...], 1, 1)
    new_oth = dot(gate_grad, wg_oth[...], 1, 1) + dot(up_grad, wu_oth[...], 1, 1)

    @pl.when(step == 0)
    def _():
        acc_own[...] = new_own
        acc_oth[...] = new_oth

    @pl.when(step > 0)
    def _():
        acc_own[...] += new_own
        acc_oth[...] += new_oth

    @pl.when(step == pl.num_programs(0) - 1)
    def _():
        start = 0
        first = 0
        copies = []
        for planes in chunks:
            count = len(planes)
            slots = groups * count * CAP
            row = lax.broadcasted_iota(jnp.int32, (2 * slots, slots), 0)
            col = lax.broadcasted_iota(jnp.int32, (2 * slots, slots), 1)
            same = ((row >> 3) == (col >> 2)) & ((row & 3) == (col & 3))
            upper = (row >> 2) & 1
            put_own = (same & (upper == rep)).astype(F32).astype(BF)
            put_oth = (same & (upper != rep)).astype(F32).astype(BF)
            mixed = dot(put_own, acc_own[start : start + slots].astype(BF), 1, 0) + dot(
                put_oth, acc_oth[start : start + slots].astype(BF), 1, 0
            )
            stage[:, first : first + count] = mixed.astype(BF).reshape(
                groups, count, 2 * CAP, HALF
            )
            for index, plane in enumerate(planes):
                copy = pltpu.make_async_copy(
                    stage.at[:, first + index],
                    back.at[:, lax.rem(place - plane + RING, RING)],
                    sems.at[first + index],
                )
                copy.start()
                copies.append(copy)
            start += slots
            first += count
        for copy in copies:
            copy.wait()


def experts(chunks, groups, place, base, recvs, weights):
    planes = sum(len(chunk) for chunk in chunks)
    slots = groups * planes * CAP
    hidden = weights[0].shape[1]
    wide = pl.BlockSpec((HALF, HTILE), lambda h: (0, h))
    tall = pl.BlockSpec((HTILE, HALF), lambda h: (h, 0))
    rows = pl.BlockSpec((slots, HALF), lambda h: (0, 0))
    tile = pl.BlockSpec((slots, HTILE), lambda h: (0, h))
    has_base = base is not None
    bases = far_memory([base]) if has_base else []
    return pl.pallas_call(
        functools.partial(expert_kernel, chunks, groups, has_base),
        grid=(hidden // HTILE,),
        out_shape=(
            [pltpu.HBM((slots, HALF), BF)] * 4
            + [pltpu.HBM((slots, hidden), BF)] * 3
            + [pltpu.HBM((groups, RING, 2 * CAP, HALF), BF)]
        ),
        in_specs=[pl.BlockSpec(memory_space=pltpu.SMEM)]
        + [pl.BlockSpec(memory_space=pl.ANY) for _ in bases]
        + [
            pl.BlockSpec(r.shape, lambda h: (0, 0, 0, 0), pipeline_mode=pl.Buffered(1))
            for r in recvs
        ]
        + [wide] * 4
        + [tall] * 2,
        out_specs=[rows] * 4 + [tile] * 3 + [pl.BlockSpec(memory_space=pl.ANY)],
        scratch_shapes=[
            pltpu.VMEM((slots, HALF), F32),
            pltpu.VMEM((slots, HALF), F32),
            pltpu.VMEM((groups, planes, 2 * CAP, HALF), BF),
            pltpu.SemaphoreType.DMA((planes,)),
        ],
        input_output_aliases={1: 7} if has_base else {},
        compiler_params=pltpu.CompilerParams(vmem_limit_bytes=EXPERT_LIMIT),
        cost_estimate=TOKEN_COST,
    )(place, *bases, *(recvs if has_base else far_memory(recvs)), *far_memory(weights))


def weight_kernel(parts, has_sum, *refs):
    xs, ss, gates, ups, hids = (refs[i * parts : (i + 1) * parts] for i in range(5))
    rest = refs[5 * parts :]
    outs = rest[-3:]

    def total(left, right):
        value = dot(left[0][...], right[0][...], 0, 0)
        for i in range(1, parts):
            value += dot(left[i][...], right[i][...], 0, 0)
        return value.astype(BF)

    for index, (left, right) in enumerate(((xs, gates), (xs, ups), (hids, ss))):
        part = total(left, right)
        if has_sum:
            part = (part.astype(F32) + rest[index][...].astype(F32)).astype(BF)
        outs[index][...] = part


def weight_grads(xs, ss, gates, ups, hids, received):
    hidden = gates[0].shape[1]
    wide = pl.BlockSpec((WTILE, hidden), lambda c: (c, 0))
    tall = pl.BlockSpec((hidden, WTILE), lambda c: (0, c))
    part_specs = [wide, wide, tall]
    narrow = [*xs, *ss]
    whole = [*gates, *ups, *hids]
    return pl.pallas_call(
        functools.partial(weight_kernel, len(xs), bool(received)),
        grid=(HALF // WTILE,),
        out_shape=[
            pltpu.HBM((HALF, hidden), BF),
            pltpu.HBM((HALF, hidden), BF),
            pltpu.HBM((hidden, HALF), BF),
        ],
        in_specs=[pl.BlockSpec((v.shape[0], WTILE), lambda c: (0, c)) for v in narrow]
        + [pl.BlockSpec(v.shape, lambda c: (0, 0)) for v in whole]
        + (part_specs if received else []),
        out_specs=part_specs,
        compiler_params=pltpu.CompilerParams(vmem_limit_bytes=VMEM_LIMIT),
        cost_estimate=TOKEN_COST,
    )(*far_memory([*narrow, *whole]), *received)


def combine_kernel(meta_ref, back_ref, out_ref):
    rows = back_ref.shape[0]
    row = lax.broadcasted_iota(jnp.int32, (rows, 128), 0)
    hit, _ = hits(by_token(meta_ref[...]), row >> 3, row & 3)
    upper = ((row >> 2) & 1) == 1
    low = (hit & ~upper).astype(F32).astype(BF)
    high = (hit & upper).astype(F32).astype(BF)
    out_ref[:, 0:HALF] = dot(low, back_ref[...], 0, 0).astype(BF)
    out_ref[:, HALF : 2 * HALF] = dot(high, back_ref[...], 0, 0).astype(BF)


def combine(packed, back):
    rows = back.shape[0]
    return pl.pallas_call(
        combine_kernel,
        grid=(1,),
        out_shape=jax.ShapeDtypeStruct((128, 2 * HALF), BF),
        in_specs=[
            pl.BlockSpec((128, META), lambda c: (0, 4 * HALF // META)),
            pl.BlockSpec((rows, HALF), lambda c: (0, 0)),
        ],
        out_specs=pl.BlockSpec((128, 2 * HALF), lambda c: (0, 0)),
        compiler_params=pltpu.CompilerParams(vmem_limit_bytes=VMEM_LIMIT),
        cost_estimate=TOKEN_COST,
    )(packed, back)


def local(inputs, out_grad, expert_ids, gates, gate_w, up_w, down_w):
    owners = lax.axis_size("expert")
    groups = owners // RING
    across = [[g * RING + z for g in range(groups)] for z in range(RING)]
    place = jnp.stack(
        [lax.rem(lax.axis_index("expert"), RING), lax.axis_index("rep")]
    ).astype(jnp.int32)

    def hop(value, by):
        pairs = [(g * RING + z, g * RING + (z + by) % RING) for g in range(groups) for z in range(RING)]
        return lax.ppermute(value, "expert", pairs)

    def swap(value):
        return lax.ppermute(value, "rep", [(0, 1), (1, 0)])

    packed = pack(inputs, out_grad, expert_ids, gates)
    data = {0: packed, 1: hop(packed, 1), -1: hop(packed, -1)}
    own = (gate_w[0], up_w[0], down_w[0])
    oth = tuple(swap(w) for w in own)
    weights = (own[0], oth[0], own[1], oth[1], own[2], oth[2])

    def near(planes, after):
        jobs = tuple((i, 0, 0, groups, 0, 0, i) for i in range(len(planes)))
        (sent,) = build(
            jobs,
            place,
            [data[p] for p in planes],
            [(groups, len(planes))],
            after,
        )
        return sent

    def exchange(sent):
        return lax.all_to_all(
            sent, "expert", split_axis=0, concat_axis=0, tiled=True, axis_index_groups=across
        )

    recv_own = exchange(near(CHUNKS[0], ()))
    recv_own, data[1], data[-1] = lax.optimization_barrier((recv_own, data[1], data[-1]))
    for by in (1, -1):
        data[2 * by] = hop(data[by], by)
    recv_next = exchange(near(CHUNKS[1], ()))
    half = groups // 2
    far = build(
        (
            (0, 1, 0, groups, 0, 0, 0),
            (0, 2, 0, half, 0, groups, 0),
            (1, -1, 0, groups, 1, 0, 0),
            (1, -2, half, groups - half, 1, groups, 0),
        ),
        place,
        [data[2], data[-2]],
        [(groups + half, 1), (2 * groups - half, 1)],
        (),
    )
    third = (hop(far[0], 1), hop(far[1], -1))
    recv_second = exchange(near(CHUNKS[2], far_memory([far[0], recv_next])))
    fourth = (hop(third[0][groups:], 1), hop(third[1][groups:], -1))
    recv_far = exchange(join(third, fourth, groups, recv_second))
    *early, back = experts(
        CHUNKS[:3], groups, place, None, (recv_own, recv_next, recv_second), weights
    )
    *late, back = experts(CHUNKS[3:], groups, place, back, (recv_far,), weights)
    x_own, x_oth, s_own, s_oth, hid, gate_grad, up_grad = zip(early, late)
    returned = lax.all_to_all(
        back.reshape(owners, 2 * CAP, HALF), "expert", split_axis=0, concat_axis=0, tiled=True
    )
    theirs = weight_grads(x_oth, s_oth, gate_grad, up_grad, hid, ())
    received = tuple(swap(part) for part in theirs)
    grads = weight_grads(x_own, s_own, gate_grad, up_grad, hid, received)
    input_grad = combine(packed, returned.reshape(owners * 2 * CAP, HALF))
    return (input_grad, grads[0][None], grads[1][None], grads[2][None])


def solution(mesh):
    return jax.shard_map(
        local,
        mesh=mesh,
        in_specs=(
            P(("expert", "rep"), None),
            P(("expert", "rep"), None),
            P(("expert", "rep"), None),
            P(("expert", "rep"), None),
            P("expert", "rep", None),
            P("expert", "rep", None),
            P("expert", None, "rep"),
        ),
        out_specs=(
            P(("expert", "rep"), None),
            P("expert", "rep", None),
            P("expert", "rep", None),
            P("expert", None, "rep"),
        ),
        check_vma=False,
    )
```

```python
import functools

import jax
import jax.numpy as jnp
from jax import lax
from jax.experimental import pallas as pl
from jax.experimental.pallas import tpu as pltpu
from jax.sharding import PartitionSpec as P

RING = 8
CAP = 4
META = 128
EXPERT_LIMIT = 40 * 1024 * 1024
HALF = 1024
COLS = 1024
WTILE = 256
CHUNKS = ((0,), (1, -1), (2, -2), (3, -3, 4))
BF = jnp.bfloat16
F32 = jnp.float32
VMEM_LIMIT = 32 * 1024 * 1024
TOKEN_COST = pl.CostEstimate(flops=1, bytes_accessed=1, transcendentals=0)


def far_memory(values):
    return [pltpu.with_memory_space_constraint(value, pltpu.HBM) for value in values]


def dot(a, b, ca, cb):
    return lax.dot_general(a, b, (((ca,), (cb,)), ((), ())), preferred_element_type=F32)


def by_token(columns):
    tokens = columns.shape[0]
    same = lax.broadcasted_iota(jnp.int32, (tokens, tokens), 0) == lax.broadcasted_iota(
        jnp.int32, (tokens, tokens), 1
    )
    return dot(columns, same.astype(F32).astype(BF), 0, 0)


def hits(meta, owner, slot):
    tokens = meta.shape[1]
    first = owner == meta[0:1, :].astype(jnp.int32)
    second = owner == meta[1:2, :].astype(jnp.int32)
    named = (first | second).astype(F32).astype(BF)
    before = (
        lax.broadcasted_iota(jnp.int32, (tokens, tokens), 0)
        < lax.broadcasted_iota(jnp.int32, (tokens, tokens), 1)
    )
    rank = dot(named, before.astype(F32).astype(BF), 1, 0)
    hit = (first | second) & (rank.astype(jnp.int32) == slot)
    gate_first = meta[2:3, :] + meta[3:4, :] + meta[4:5, :]
    gate_second = meta[5:6, :] + meta[6:7, :] + meta[7:8, :]
    gate = jnp.where(first, gate_first, 0.0) + jnp.where(second, gate_second, 0.0)
    return hit, jnp.sum(jnp.where(hit, gate, 0.0), axis=1, keepdims=True)


def pack_kernel(x_ref, grad_ref, ids_ref, gates_ref, out_ref):
    width = x_ref.shape[1]
    tokens = x_ref.shape[0]
    out_ref[:, 0:width] = x_ref[...]
    out_ref[:, width : 2 * width] = grad_ref[...]
    lane = lax.broadcasted_iota(jnp.int32, (tokens, META), 1)
    packed = jnp.zeros((tokens, META), F32)
    for k in range(2):
        packed = jnp.where(lane == k, ids_ref[:, k : k + 1].astype(F32), packed)
        rest = gates_ref[:, k : k + 1]
        for part in range(3):
            piece = rest.astype(BF).astype(F32)
            packed = jnp.where(lane == 2 + 3 * k + part, piece, packed)
            rest = rest - piece
    out_ref[:, 2 * width :] = packed.astype(BF)


def pack(x, grad, ids, gates):
    return pl.pallas_call(
        pack_kernel,
        out_shape=jax.ShapeDtypeStruct((x.shape[0], 2 * x.shape[1] + META), BF),
        compiler_params=pltpu.CompilerParams(vmem_limit_bytes=VMEM_LIMIT),
        cost_estimate=TOKEN_COST,
    )(*far_memory([x, grad]), ids, gates)


def build_kernel(jobs, sources, outs, waits, place_ref, *refs):
    refs = refs[waits:]
    metas, data = refs[:sources], refs[sources : 3 * sources]
    out_refs, picks = refs[3 * sources : 3 * sources + outs], refs[3 * sources + outs :]
    place = place_ref[0]

    @pl.when(pl.program_id(0) == 0)
    def _():
        by = [by_token(meta[...]) for meta in metas]
        for number, (source, offset, start, groups, _, _, _) in enumerate(jobs):
            pick, scale = picks[2 * number], picks[2 * number + 1]
            row = lax.broadcasted_iota(jnp.int32, (groups * 2 * CAP, 128), 0)
            owner = ((row >> 3) + start) * RING + lax.rem(place + offset + RING, RING)
            is_grad = ((row >> 2) & 1) == 1
            hit, gate = hits(by[source], owner, row & 3)
            pick[:, 0:128] = (hit & ~is_grad).astype(F32).astype(BF)
            pick[:, 128:256] = (hit & is_grad).astype(F32).astype(BF)
            scale[...] = jnp.where(is_grad, gate, 1.0)

    for number, (source, _, _, groups, out, to, at) in enumerate(jobs):
        stacked = jnp.concatenate([data[2 * source][...], data[2 * source + 1][...]], axis=0)
        value = dot(picks[2 * number][...], stacked, 1, 0) * picks[2 * number + 1][:, 0:1]
        out_refs[out][to : to + groups, at] = value.astype(BF).reshape(
            groups, 2 * CAP, value.shape[1]
        )


def build(jobs, place, planes, shapes, after=()):
    features = (planes[0].shape[1] - META) // 2
    sources = len(planes)
    tokens = planes[0].shape[0]
    steps = features // COLS
    scratch = []
    for job in jobs:
        rows = job[3] * 2 * CAP
        scratch += [pltpu.VMEM((rows, 256), BF), pltpu.VMEM((rows, 128), F32)]
    shapes = [shape + (2 * CAP,) for shape in shapes]
    return pl.pallas_call(
        functools.partial(build_kernel, jobs, sources, len(shapes), len(after)),
        grid=(steps,),
        out_shape=[pltpu.HBM(shape + (features,), BF) for shape in shapes],
        in_specs=[pl.BlockSpec(memory_space=pltpu.SMEM)]
        + [pl.BlockSpec(memory_space=pl.ANY) for _ in after]
        + [pl.BlockSpec((tokens, META), lambda c: (0, 2 * features // META))] * sources
        + [
            pl.BlockSpec((tokens, COLS), lambda c: (0, c)),
            pl.BlockSpec((tokens, COLS), lambda c: (0, c + steps)),
        ]
        * sources,
        out_specs=[pl.BlockSpec(shape + (COLS,), lambda c: (0, 0, 0, c)) for shape in shapes],
        scratch_shapes=scratch,
        compiler_params=pltpu.CompilerParams(vmem_limit_bytes=VMEM_LIMIT),
        cost_estimate=TOKEN_COST,
    )(place, *after, *planes, *[p for p in planes for _ in range(2)])


def join_kernel(left_ref, right_ref, far_left_ref, far_right_ref, after_ref, out_ref):
    del after_ref
    half = far_left_ref.shape[0]
    out_ref[:, 0:1] = left_ref[...]
    out_ref[:, 1:2] = right_ref[...]
    out_ref[0:half, 2:3] = far_left_ref[...]
    out_ref[half:, 2:3] = far_right_ref[...]


def join(third, fourth, groups, after):
    features = third[0].shape[3]
    shape = (groups, 1, 2 * CAP)
    specs = [pl.BlockSpec(shape + (COLS,), lambda c: (0, 0, 0, c))] * 2
    specs += [pl.BlockSpec(v.shape[:3] + (COLS,), lambda c: (0, 0, 0, c)) for v in fourth]
    return pl.pallas_call(
        join_kernel,
        grid=(features // COLS,),
        out_shape=pltpu.HBM((groups, 3, 2 * CAP, features), BF),
        in_specs=specs + [pl.BlockSpec(memory_space=pl.ANY)],
        out_specs=pl.BlockSpec((groups, 3, 2 * CAP, COLS), lambda c: (0, 0, 0, c)),
        compiler_params=pltpu.CompilerParams(vmem_limit_bytes=VMEM_LIMIT),
        cost_estimate=TOKEN_COST,
    )(*third, *fourth, after)


def expert_kernel(chunks, groups, has_base, place_ref, *refs):
    refs = refs[1:] if has_base else refs
    recvs, refs = refs[: len(chunks)], refs[len(chunks) :]
    sources, results, back = refs[:6], refs[6:13], refs[13]
    held, refs = refs[14:20], refs[20:]
    x_own, x_oth, s_own, s_oth, hid_ref, gg_ref, ug_ref = refs[:7]
    stage, load_sems, store_sems, back_sems = refs[7:]
    wg_own, wg_oth, wu_own, wu_oth, wd_own, wd_oth = held
    place = place_ref[0]
    rep = place_ref[1]
    loads = [
        pltpu.make_async_copy(sources[i], held[i], load_sems.at[i]) for i in range(len(held))
    ]
    stores = [
        pltpu.make_async_copy(refs[i], results[i], store_sems.at[i]) for i in range(len(results))
    ]
    for load in loads:
        load.start()
    start = 0
    for recv, planes in zip(recvs, chunks):
        slots = groups * len(planes) * CAP
        row = lax.broadcasted_iota(jnp.int32, (2 * slots, 2 * slots), 0)
        col = lax.broadcasted_iota(jnp.int32, (2 * slots, 2 * slots), 1)
        grad = (row >= slots).astype(jnp.int32)
        inner = row - slots * grad
        take = (col == (inner >> 2) * 8 + (inner & 3) + 4 * grad).astype(F32).astype(BF)
        for half, x_ref, s_ref in ((rep, x_own, s_own), (1 - rep, x_oth, s_oth)):
            at = pl.ds(pl.multiple_of(half * HALF, HALF), HALF)
            both = dot(take, recv[:, :, :, at].reshape(2 * slots, HALF), 1, 0).astype(BF)
            x_ref[start : start + slots] = both[:slots]
            s_ref[start : start + slots] = both[slots:]
        start += slots
    for store in stores[:4]:
        store.start()
    for load in loads[:2]:
        load.wait()
    gate = dot(x_own[...], wg_own[...], 1, 0) + dot(x_oth[...], wg_oth[...], 1, 0)
    for load in loads[2:4]:
        load.wait()
    up = dot(x_own[...], wu_own[...], 1, 0) + dot(x_oth[...], wu_oth[...], 1, 0)
    sigma = jax.nn.sigmoid(gate)
    silu = gate * sigma
    hid_ref[...] = (silu * up).astype(BF)
    for load in loads[4:]:
        load.wait()
    hidden_grad = dot(s_own[...], wd_own[...], 1, 1) + dot(s_oth[...], wd_oth[...], 1, 1)
    gg_ref[...] = (hidden_grad * up * sigma * (1.0 + gate * (1.0 - sigma))).astype(BF)
    ug_ref[...] = (hidden_grad * silu).astype(BF)
    for store in stores[4:]:
        store.start()
    slot_own = dot(gg_ref[...], wg_own[...], 1, 1) + dot(ug_ref[...], wu_own[...], 1, 1)
    slot_own = slot_own.astype(BF)
    slot_oth = dot(gg_ref[...], wg_oth[...], 1, 1) + dot(ug_ref[...], wu_oth[...], 1, 1)
    slot_oth = slot_oth.astype(BF)
    start = 0
    first = 0
    copies = []
    for planes in chunks:
        count = len(planes)
        slots = groups * count * CAP
        row = lax.broadcasted_iota(jnp.int32, (2 * slots, slots), 0)
        col = lax.broadcasted_iota(jnp.int32, (2 * slots, slots), 1)
        same = ((row >> 3) == (col >> 2)) & ((row & 3) == (col & 3))
        upper = (row >> 2) & 1
        put_own = (same & (upper == rep)).astype(F32).astype(BF)
        put_oth = (same & (upper != rep)).astype(F32).astype(BF)
        mixed = dot(put_own, slot_own[start : start + slots], 1, 0) + dot(
            put_oth, slot_oth[start : start + slots], 1, 0
        )
        stage[:, first : first + count] = mixed.astype(BF).reshape(groups, count, 2 * CAP, HALF)
        for index, plane in enumerate(planes):
            copy = pltpu.make_async_copy(
                stage.at[:, first + index],
                back.at[:, lax.rem(place - plane + RING, RING)],
                back_sems.at[first + index],
            )
            copy.start()
            copies.append(copy)
        start += slots
        first += count
    for copy in copies + stores:
        copy.wait()


def experts(chunks, groups, place, base, recvs, weights):
    planes = sum(len(chunk) for chunk in chunks)
    slots = groups * planes * CAP
    hidden = weights[0].shape[1]
    has_base = base is not None
    bases = far_memory([base]) if has_base else []
    anywhere = pl.BlockSpec(memory_space=pl.ANY)
    return pl.pallas_call(
        functools.partial(expert_kernel, chunks, groups, has_base),
        out_shape=(
            [pltpu.HBM((slots, HALF), BF)] * 4
            + [pltpu.HBM((slots, hidden), BF)] * 3
            + [pltpu.HBM((groups, RING, 2 * CAP, HALF), BF)]
        ),
        in_specs=[pl.BlockSpec(memory_space=pltpu.SMEM)]
        + [anywhere for _ in bases]
        + [pl.BlockSpec(memory_space=pltpu.VMEM) for _ in recvs]
        + [anywhere] * 6,
        out_specs=[anywhere] * 8,
        scratch_shapes=[pltpu.VMEM(w.shape, BF) for w in weights]
        + [pltpu.VMEM((slots, HALF), BF)] * 4
        + [pltpu.VMEM((slots, hidden), BF)] * 3
        + [
            pltpu.VMEM((groups, planes, 2 * CAP, HALF), BF),
            pltpu.SemaphoreType.DMA((6,)),
            pltpu.SemaphoreType.DMA((7,)),
            pltpu.SemaphoreType.DMA((planes,)),
        ],
        input_output_aliases={1: 7} if has_base else {},
        compiler_params=pltpu.CompilerParams(vmem_limit_bytes=EXPERT_LIMIT),
        cost_estimate=TOKEN_COST,
    )(place, *bases, *recvs, *far_memory(weights))


def weight_kernel(parts, has_sum, *refs):
    xs, ss, gates, ups, hids = (refs[i * parts : (i + 1) * parts] for i in range(5))
    rest = refs[5 * parts :]
    outs = rest[-3:]

    def total(left, right):
        value = dot(left[0][...], right[0][...], 0, 0)
        for i in range(1, parts):
            value += dot(left[i][...], right[i][...], 0, 0)
        return value.astype(BF)

    for index, (left, right) in enumerate(((xs, gates), (xs, ups), (hids, ss))):
        part = total(left, right)
        if has_sum:
            part = (part.astype(F32) + rest[index][...].astype(F32)).astype(BF)
        outs[index][...] = part


def weight_grads(xs, ss, gates, ups, hids, received):
    hidden = gates[0].shape[1]
    wide = pl.BlockSpec((WTILE, hidden), lambda c: (c, 0))
    tall = pl.BlockSpec((hidden, WTILE), lambda c: (0, c))
    part_specs = [wide, wide, tall]
    narrow = [*xs, *ss]
    whole = [*gates, *ups, *hids]
    return pl.pallas_call(
        functools.partial(weight_kernel, len(xs), bool(received)),
        grid=(HALF // WTILE,),
        out_shape=[
            pltpu.HBM((HALF, hidden), BF),
            pltpu.HBM((HALF, hidden), BF),
            pltpu.HBM((hidden, HALF), BF),
        ],
        in_specs=[pl.BlockSpec((v.shape[0], WTILE), lambda c: (0, c)) for v in narrow]
        + [pl.BlockSpec(v.shape, lambda c: (0, 0)) for v in whole]
        + (part_specs if received else []),
        out_specs=part_specs,
        compiler_params=pltpu.CompilerParams(vmem_limit_bytes=VMEM_LIMIT),
        cost_estimate=TOKEN_COST,
    )(*far_memory([*narrow, *whole]), *received)


def combine_kernel(meta_ref, back_ref, out_ref):
    rows = back_ref.shape[0]
    row = lax.broadcasted_iota(jnp.int32, (rows, 128), 0)
    hit, _ = hits(by_token(meta_ref[...]), row >> 3, row & 3)
    upper = ((row >> 2) & 1) == 1
    low = (hit & ~upper).astype(F32).astype(BF)
    high = (hit & upper).astype(F32).astype(BF)
    out_ref[:, 0:HALF] = dot(low, back_ref[...], 0, 0).astype(BF)
    out_ref[:, HALF : 2 * HALF] = dot(high, back_ref[...], 0, 0).astype(BF)


def combine(packed, back):
    rows = back.shape[0]
    return pl.pallas_call(
        combine_kernel,
        grid=(1,),
        out_shape=jax.ShapeDtypeStruct((128, 2 * HALF), BF),
        in_specs=[
            pl.BlockSpec((128, META), lambda c: (0, 4 * HALF // META)),
            pl.BlockSpec((rows, HALF), lambda c: (0, 0)),
        ],
        out_specs=pl.BlockSpec((128, 2 * HALF), lambda c: (0, 0)),
        compiler_params=pltpu.CompilerParams(vmem_limit_bytes=VMEM_LIMIT),
        cost_estimate=TOKEN_COST,
    )(packed, back)


def local(inputs, out_grad, expert_ids, gates, gate_w, up_w, down_w):
    owners = lax.axis_size("expert")
    groups = owners // RING
    across = [[g * RING + z for g in range(groups)] for z in range(RING)]
    place = jnp.stack(
        [lax.rem(lax.axis_index("expert"), RING), lax.axis_index("rep")]
    ).astype(jnp.int32)

    def hop(value, by):
        pairs = [(g * RING + z, g * RING + (z + by) % RING) for g in range(groups) for z in range(RING)]
        return lax.ppermute(value, "expert", pairs)

    def swap(value):
        return lax.ppermute(value, "rep", [(0, 1), (1, 0)])

    packed = pack(inputs, out_grad, expert_ids, gates)
    data = {0: packed, 1: hop(packed, 1), -1: hop(packed, -1)}
    own = (gate_w[0], up_w[0], down_w[0])
    oth = tuple(swap(w) for w in own)
    weights = (own[0], oth[0], own[1], oth[1], own[2], oth[2])

    def near(planes, after):
        jobs = tuple((i, 0, 0, groups, 0, 0, i) for i in range(len(planes)))
        (sent,) = build(
            jobs,
            place,
            far_memory([data[p] for p in planes]) if planes == CHUNKS[1] else [data[p] for p in planes],
            [(groups, len(planes))],
            after,
        )
        return sent

    def exchange(sent):
        return lax.all_to_all(
            sent, "expert", split_axis=0, concat_axis=0, tiled=True, axis_index_groups=across
        )

    recv_own = exchange(near(CHUNKS[0], ()))
    recv_own, data[1], data[-1] = lax.optimization_barrier((recv_own, data[1], data[-1]))
    for by in (1, -1):
        data[2 * by] = hop(data[by], by)
    recv_next = exchange(near(CHUNKS[1], ()))
    half = groups // 2
    far = build(
        (
            (0, 1, 0, groups, 0, 0, 0),
            (0, 2, 0, half, 0, groups, 0),
            (1, -1, 0, groups, 1, 0, 0),
            (1, -2, half, groups - half, 1, groups, 0),
        ),
        place,
        [data[2], data[-2]],
        [(groups + half, 1), (2 * groups - half, 1)],
        (),
    )
    third = (hop(far[0], 1), hop(far[1], -1))
    recv_second = exchange(near(CHUNKS[2], far_memory([far[0], recv_next])))
    fourth = (hop(third[0][groups:], 1), hop(third[1][groups:], -1))
    recv_far = exchange(join(third, fourth, groups, recv_second))
    *early, back = experts(
        CHUNKS[:3], groups, place, None, (recv_own, recv_next, recv_second), weights
    )
    *late, back = experts(CHUNKS[3:], groups, place, back, (recv_far,), weights)
    x_own, x_oth, s_own, s_oth, hid, gate_grad, up_grad = zip(early, late)
    returned = lax.all_to_all(
        back.reshape(owners, 2 * CAP, HALF), "expert", split_axis=0, concat_axis=0, tiled=True
    )
    theirs = weight_grads(x_oth, s_oth, gate_grad, up_grad, hid, ())
    received = tuple(swap(part) for part in theirs)
    grads = weight_grads(x_own, s_own, gate_grad, up_grad, hid, received)
    input_grad = combine(packed, returned.reshape(owners * 2 * CAP, HALF))
    return (input_grad, grads[0][None], grads[1][None], grads[2][None])


def solution(mesh):
    return jax.shard_map(
        local,
        mesh=mesh,
        in_specs=(
            P(("expert", "rep"), None),
            P(("expert", "rep"), None),
            P(("expert", "rep"), None),
            P(("expert", "rep"), None),
            P("expert", "rep", None),
            P("expert", "rep", None),
            P("expert", None, "rep"),
        ),
        out_specs=(
            P(("expert", "rep"), None),
            P("expert", "rep", None),
            P("expert", "rep", None),
            P("expert", None, "rep"),
        ),
        check_vma=False,
    )
```

```python
import functools

import jax
import jax.numpy as jnp
from jax import lax
from jax.experimental import pallas as pl
from jax.experimental.pallas import tpu as pltpu
from jax.sharding import PartitionSpec as P

RING = 8
CAP = 4
META = 128
EXPERT_LIMIT = 40 * 1024 * 1024
HALF = 1024
COLS = 1024
WTILE = 256
CHUNKS = ((0,), (1, -1), (2, -2), (3, -3, 4))
BF = jnp.bfloat16
F32 = jnp.float32
VMEM_LIMIT = 32 * 1024 * 1024
TOKEN_COST = pl.CostEstimate(flops=1, bytes_accessed=1, transcendentals=0)


def far_memory(values):
    return [pltpu.with_memory_space_constraint(value, pltpu.HBM) for value in values]


def dot(a, b, ca, cb):
    return lax.dot_general(a, b, (((ca,), (cb,)), ((), ())), preferred_element_type=F32)


def by_token(columns):
    tokens = columns.shape[0]
    same = lax.broadcasted_iota(jnp.int32, (tokens, tokens), 0) == lax.broadcasted_iota(
        jnp.int32, (tokens, tokens), 1
    )
    return dot(columns, same.astype(F32).astype(BF), 0, 0)


def hits(meta, owner, slot):
    tokens = meta.shape[1]
    first = owner == meta[0:1, :].astype(jnp.int32)
    second = owner == meta[1:2, :].astype(jnp.int32)
    named = (first | second).astype(F32).astype(BF)
    before = (
        lax.broadcasted_iota(jnp.int32, (tokens, tokens), 0)
        < lax.broadcasted_iota(jnp.int32, (tokens, tokens), 1)
    )
    rank = dot(named, before.astype(F32).astype(BF), 1, 0)
    hit = (first | second) & (rank.astype(jnp.int32) == slot)
    gate_first = meta[2:3, :] + meta[3:4, :] + meta[4:5, :]
    gate_second = meta[5:6, :] + meta[6:7, :] + meta[7:8, :]
    gate = jnp.where(first, gate_first, 0.0) + jnp.where(second, gate_second, 0.0)
    return hit, jnp.sum(jnp.where(hit, gate, 0.0), axis=1, keepdims=True)


def pack_kernel(x_ref, grad_ref, ids_ref, gates_ref, out_ref):
    width = x_ref.shape[1]
    tokens = x_ref.shape[0]
    out_ref[:, 0:width] = x_ref[...]
    out_ref[:, width : 2 * width] = grad_ref[...]
    row = lax.broadcasted_iota(jnp.int32, (META, tokens), 0)
    packed = jnp.zeros((META, tokens), F32)
    for k in range(2):
        packed = jnp.where(row == k, ids_ref[k : k + 1, :].astype(F32), packed)
        rest = gates_ref[k : k + 1, :]
        for part in range(3):
            piece = rest.astype(BF).astype(F32)
            packed = jnp.where(row == 2 + 3 * k + part, piece, packed)
            rest = rest - piece
    same = lax.broadcasted_iota(jnp.int32, (tokens, tokens), 0) == lax.broadcasted_iota(
        jnp.int32, (tokens, tokens), 1
    )
    columns = dot(same.astype(F32).astype(BF), packed.astype(BF), 1, 1)
    out_ref[:, 2 * width :] = columns.astype(BF)


def pack(x, grad, ids, gates):
    return pl.pallas_call(
        pack_kernel,
        out_shape=jax.ShapeDtypeStruct((x.shape[0], 2 * x.shape[1] + META), BF),
        compiler_params=pltpu.CompilerParams(vmem_limit_bytes=VMEM_LIMIT),
        cost_estimate=TOKEN_COST,
    )(*far_memory([x, grad, ids, gates]))


def build_kernel(jobs, sources, outs, waits, place_ref, *refs):
    refs = refs[waits:]
    metas, data = refs[:sources], refs[sources : 3 * sources]
    out_refs, picks = refs[3 * sources : 3 * sources + outs], refs[3 * sources + outs :]
    place = place_ref[0]

    @pl.when(pl.program_id(0) == 0)
    def _():
        by = [by_token(meta[...]) for meta in metas]
        for number, (source, offset, start, groups, _, _, _) in enumerate(jobs):
            pick, scale = picks[2 * number], picks[2 * number + 1]
            row = lax.broadcasted_iota(jnp.int32, (groups * 2 * CAP, 128), 0)
            owner = ((row >> 3) + start) * RING + lax.rem(place + offset + RING, RING)
            is_grad = ((row >> 2) & 1) == 1
            hit, gate = hits(by[source], owner, row & 3)
            pick[:, 0:128] = (hit & ~is_grad).astype(F32).astype(BF)
            pick[:, 128:256] = (hit & is_grad).astype(F32).astype(BF)
            scale[...] = jnp.where(is_grad, gate, 1.0)

    for number, (source, _, _, groups, out, to, at) in enumerate(jobs):
        stacked = jnp.concatenate([data[2 * source][...], data[2 * source + 1][...]], axis=0)
        value = dot(picks[2 * number][...], stacked, 1, 0) * picks[2 * number + 1][:, 0:1]
        out_refs[out][to : to + groups, at] = value.astype(BF).reshape(
            groups, 2 * CAP, value.shape[1]
        )


def build(jobs, place, planes, shapes, after=()):
    features = (planes[0].shape[1] - META) // 2
    sources = len(planes)
    tokens = planes[0].shape[0]
    steps = features // COLS
    scratch = []
    for job in jobs:
        rows = job[3] * 2 * CAP
        scratch += [pltpu.VMEM((rows, 256), BF), pltpu.VMEM((rows, 128), F32)]
    shapes = [shape + (2 * CAP,) for shape in shapes]
    return pl.pallas_call(
        functools.partial(build_kernel, jobs, sources, len(shapes), len(after)),
        grid=(steps,),
        out_shape=[pltpu.HBM(shape + (features,), BF) for shape in shapes],
        in_specs=[pl.BlockSpec(memory_space=pltpu.SMEM)]
        + [pl.BlockSpec(memory_space=pl.ANY) for _ in after]
        + [pl.BlockSpec((tokens, META), lambda c: (0, 2 * features // META))] * sources
        + [
            pl.BlockSpec((tokens, COLS), lambda c: (0, c)),
            pl.BlockSpec((tokens, COLS), lambda c: (0, c + steps)),
        ]
        * sources,
        out_specs=[pl.BlockSpec(shape + (COLS,), lambda c: (0, 0, 0, c)) for shape in shapes],
        scratch_shapes=scratch,
        compiler_params=pltpu.CompilerParams(vmem_limit_bytes=VMEM_LIMIT),
        cost_estimate=TOKEN_COST,
    )(place, *after, *planes, *[p for p in planes for _ in range(2)])


def join_kernel(left_ref, right_ref, far_left_ref, far_right_ref, after_ref, out_ref):
    del after_ref
    half = far_left_ref.shape[0]
    out_ref[:, 0:1] = left_ref[...]
    out_ref[:, 1:2] = right_ref[...]
    out_ref[0:half, 2:3] = far_left_ref[...]
    out_ref[half:, 2:3] = far_right_ref[...]


def join(third, fourth, groups, after):
    features = third[0].shape[3]
    shape = (groups, 1, 2 * CAP)
    specs = [pl.BlockSpec(shape + (COLS,), lambda c: (0, 0, 0, c))] * 2
    specs += [pl.BlockSpec(v.shape[:3] + (COLS,), lambda c: (0, 0, 0, c)) for v in fourth]
    return pl.pallas_call(
        join_kernel,
        grid=(features // COLS,),
        out_shape=pltpu.HBM((groups, 3, 2 * CAP, features), BF),
        in_specs=specs + [pl.BlockSpec(memory_space=pl.ANY)],
        out_specs=pl.BlockSpec((groups, 3, 2 * CAP, COLS), lambda c: (0, 0, 0, c)),
        compiler_params=pltpu.CompilerParams(vmem_limit_bytes=VMEM_LIMIT),
        cost_estimate=TOKEN_COST,
    )(*third, *fourth, after)


def expert_kernel(chunks, groups, has_base, place_ref, *refs):
    refs = refs[1:] if has_base else refs
    recvs, refs = refs[: len(chunks)], refs[len(chunks) :]
    sources, results, back = refs[:6], refs[6:13], refs[13]
    held, refs = refs[14:20], refs[20:]
    x_own, x_oth, s_own, s_oth, hid_ref, gg_ref, ug_ref = refs[:7]
    stage, load_sems, store_sems, back_sems = refs[7:]
    wg_own, wg_oth, wu_own, wu_oth, wd_own, wd_oth = held
    place = place_ref[0]
    rep = place_ref[1]
    loads = [
        pltpu.make_async_copy(sources[i], held[i], load_sems.at[i]) for i in range(len(held))
    ]
    stores = [
        pltpu.make_async_copy(refs[i], results[i], store_sems.at[i]) for i in range(len(results))
    ]
    for load in loads:
        load.start()
    start = 0
    for recv, planes in zip(recvs, chunks):
        slots = groups * len(planes) * CAP
        row = lax.broadcasted_iota(jnp.int32, (2 * slots, 2 * slots), 0)
        col = lax.broadcasted_iota(jnp.int32, (2 * slots, 2 * slots), 1)
        grad = (row >= slots).astype(jnp.int32)
        inner = row - slots * grad
        take = (col == (inner >> 2) * 8 + (inner & 3) + 4 * grad).astype(F32).astype(BF)
        for half, x_ref, s_ref in ((rep, x_own, s_own), (1 - rep, x_oth, s_oth)):
            at = pl.ds(pl.multiple_of(half * HALF, HALF), HALF)
            both = dot(take, recv[:, :, :, at].reshape(2 * slots, HALF), 1, 0).astype(BF)
            x_ref[start : start + slots] = both[:slots]
            s_ref[start : start + slots] = both[slots:]
        start += slots
    for store in stores[:4]:
        store.start()
    for load in loads[:2]:
        load.wait()
    gate = dot(x_own[...], wg_own[...], 1, 0) + dot(x_oth[...], wg_oth[...], 1, 0)
    for load in loads[2:4]:
        load.wait()
    up = dot(x_own[...], wu_own[...], 1, 0) + dot(x_oth[...], wu_oth[...], 1, 0)
    sigma = jax.nn.sigmoid(gate)
    silu = gate * sigma
    hid_ref[...] = (silu * up).astype(BF)
    for load in loads[4:]:
        load.wait()
    hidden_grad = dot(s_own[...], wd_own[...], 1, 1) + dot(s_oth[...], wd_oth[...], 1, 1)
    gg_ref[...] = (hidden_grad * up * sigma * (1.0 + gate * (1.0 - sigma))).astype(BF)
    ug_ref[...] = (hidden_grad * silu).astype(BF)
    for store in stores[4:]:
        store.start()
    slot_own = dot(gg_ref[...], wg_own[...], 1, 1) + dot(ug_ref[...], wu_own[...], 1, 1)
    slot_own = slot_own.astype(BF)
    slot_oth = dot(gg_ref[...], wg_oth[...], 1, 1) + dot(ug_ref[...], wu_oth[...], 1, 1)
    slot_oth = slot_oth.astype(BF)
    start = 0
    first = 0
    copies = []
    for planes in chunks:
        count = len(planes)
        slots = groups * count * CAP
        row = lax.broadcasted_iota(jnp.int32, (2 * slots, slots), 0)
        col = lax.broadcasted_iota(jnp.int32, (2 * slots, slots), 1)
        same = ((row >> 3) == (col >> 2)) & ((row & 3) == (col & 3))
        upper = (row >> 2) & 1
        put_own = (same & (upper == rep)).astype(F32).astype(BF)
        put_oth = (same & (upper != rep)).astype(F32).astype(BF)
        mixed = dot(put_own, slot_own[start : start + slots], 1, 0) + dot(
            put_oth, slot_oth[start : start + slots], 1, 0
        )
        stage[:, first : first + count] = mixed.astype(BF).reshape(groups, count, 2 * CAP, HALF)
        for index, plane in enumerate(planes):
            copy = pltpu.make_async_copy(
                stage.at[:, first + index],
                back.at[:, lax.rem(place - plane + RING, RING)],
                back_sems.at[first + index],
            )
            copy.start()
            copies.append(copy)
        start += slots
        first += count
    for copy in copies + stores:
        copy.wait()


def experts(chunks, groups, place, base, recvs, weights):
    planes = sum(len(chunk) for chunk in chunks)
    slots = groups * planes * CAP
    hidden = weights[0].shape[1]
    has_base = base is not None
    bases = far_memory([base]) if has_base else []
    anywhere = pl.BlockSpec(memory_space=pl.ANY)
    return pl.pallas_call(
        functools.partial(expert_kernel, chunks, groups, has_base),
        out_shape=(
            [pltpu.HBM((slots, HALF), BF)] * 4
            + [pltpu.HBM((slots, hidden), BF)] * 3
            + [pltpu.HBM((groups, RING, 2 * CAP, HALF), BF)]
        ),
        in_specs=[pl.BlockSpec(memory_space=pltpu.SMEM)]
        + [anywhere for _ in bases]
        + [pl.BlockSpec(memory_space=pltpu.VMEM) for _ in recvs]
        + [anywhere] * 6,
        out_specs=[anywhere] * 8,
        scratch_shapes=[pltpu.VMEM(w.shape, BF) for w in weights]
        + [pltpu.VMEM((slots, HALF), BF)] * 4
        + [pltpu.VMEM((slots, hidden), BF)] * 3
        + [
            pltpu.VMEM((groups, planes, 2 * CAP, HALF), BF),
            pltpu.SemaphoreType.DMA((6,)),
            pltpu.SemaphoreType.DMA((7,)),
            pltpu.SemaphoreType.DMA((planes,)),
        ],
        input_output_aliases={1: 7} if has_base else {},
        compiler_params=pltpu.CompilerParams(vmem_limit_bytes=EXPERT_LIMIT),
        cost_estimate=TOKEN_COST,
    )(place, *bases, *recvs, *far_memory(weights))


def weight_kernel(parts, has_sum, *refs):
    xs, ss, gates, ups, hids = (refs[i * parts : (i + 1) * parts] for i in range(5))
    rest = refs[5 * parts :]
    outs = rest[-3:]

    def total(left, right):
        value = dot(left[0][...], right[0][...], 0, 0)
        for i in range(1, parts):
            value += dot(left[i][...], right[i][...], 0, 0)
        return value.astype(BF)

    for index, (left, right) in enumerate(((xs, gates), (xs, ups), (hids, ss))):
        part = total(left, right)
        if has_sum:
            part = (part.astype(F32) + rest[index][...].astype(F32)).astype(BF)
        outs[index][...] = part


def weight_grads(xs, ss, gates, ups, hids, received):
    hidden = gates[0].shape[1]
    wide = pl.BlockSpec((WTILE, hidden), lambda c: (c, 0))
    tall = pl.BlockSpec((hidden, WTILE), lambda c: (0, c))
    part_specs = [wide, wide, tall]
    narrow = [*xs, *ss]
    whole = [*gates, *ups, *hids]
    return pl.pallas_call(
        functools.partial(weight_kernel, len(xs), bool(received)),
        grid=(HALF // WTILE,),
        out_shape=[
            pltpu.HBM((HALF, hidden), BF),
            pltpu.HBM((HALF, hidden), BF),
            pltpu.HBM((hidden, HALF), BF),
        ],
        in_specs=[pl.BlockSpec((v.shape[0], WTILE), lambda c: (0, c)) for v in narrow]
        + [pl.BlockSpec(v.shape, lambda c: (0, 0)) for v in whole]
        + (part_specs if received else []),
        out_specs=part_specs,
        compiler_params=pltpu.CompilerParams(vmem_limit_bytes=VMEM_LIMIT),
        cost_estimate=TOKEN_COST,
    )(*far_memory([*narrow, *whole]), *received)


def returns_kernel(meta_ref, low_ref, high_ref):
    rows = low_ref.shape[0]
    row = lax.broadcasted_iota(jnp.int32, (rows, 128), 0)
    hit, _ = hits(by_token(meta_ref[...]), row >> 3, row & 3)
    upper = ((row >> 2) & 1) == 1
    low_ref[...] = (hit & ~upper).astype(F32).astype(BF)
    high_ref[...] = (hit & upper).astype(F32).astype(BF)


def returns(packed, owners):
    rows = owners * 2 * CAP
    whole = pl.BlockSpec((rows, 128), lambda c: (0, 0))
    return pl.pallas_call(
        returns_kernel,
        grid=(1,),
        out_shape=[jax.ShapeDtypeStruct((rows, 128), BF)] * 2,
        in_specs=[pl.BlockSpec((128, META), lambda c: (0, 4 * HALF // META))],
        out_specs=[whole, whole],
        compiler_params=pltpu.CompilerParams(vmem_limit_bytes=VMEM_LIMIT),
        cost_estimate=TOKEN_COST,
    )(packed)


def combine_kernel(low_ref, high_ref, back_ref, out_ref):
    out_ref[:, 0:HALF] = dot(low_ref[...], back_ref[...], 0, 0).astype(BF)
    out_ref[:, HALF : 2 * HALF] = dot(high_ref[...], back_ref[...], 0, 0).astype(BF)


def combine(low, high, back):
    return pl.pallas_call(
        combine_kernel,
        out_shape=jax.ShapeDtypeStruct((128, 2 * HALF), BF),
        compiler_params=pltpu.CompilerParams(vmem_limit_bytes=VMEM_LIMIT),
        cost_estimate=TOKEN_COST,
    )(low, high, back)


def local(inputs, out_grad, expert_ids, gates, gate_w, up_w, down_w):
    owners = lax.axis_size("expert")
    groups = owners // RING
    across = [[g * RING + z for g in range(groups)] for z in range(RING)]
    place = jnp.stack(
        [lax.rem(lax.axis_index("expert"), RING), lax.axis_index("rep")]
    ).astype(jnp.int32)

    def hop(value, by):
        pairs = [(g * RING + z, g * RING + (z + by) % RING) for g in range(groups) for z in range(RING)]
        return lax.ppermute(value, "expert", pairs)

    def swap(value):
        return lax.ppermute(value, "rep", [(0, 1), (1, 0)])

    packed = pack(inputs, out_grad, expert_ids.T, gates.T)
    data = {0: packed, 1: hop(packed, 1), -1: hop(packed, -1)}
    own = (gate_w[0], up_w[0], down_w[0])
    oth = tuple(swap(w) for w in own)
    weights = (own[0], oth[0], own[1], oth[1], own[2], oth[2])

    def near(planes, after):
        jobs = tuple((i, 0, 0, groups, 0, 0, i) for i in range(len(planes)))
        (sent,) = build(
            jobs,
            place,
            far_memory([data[p] for p in planes]) if planes == CHUNKS[1] else [data[p] for p in planes],
            [(groups, len(planes))],
            after,
        )
        return sent

    def exchange(sent):
        return lax.all_to_all(
            sent, "expert", split_axis=0, concat_axis=0, tiled=True, axis_index_groups=across
        )

    recv_own = exchange(near(CHUNKS[0], ()))
    recv_own, data[1], data[-1] = lax.optimization_barrier((recv_own, data[1], data[-1]))
    for by in (1, -1):
        data[2 * by] = hop(data[by], by)
    recv_next = exchange(near(CHUNKS[1], ()))
    half = groups // 2
    far = build(
        (
            (0, 1, 0, groups, 0, 0, 0),
            (0, 2, 0, half, 0, groups, 0),
            (1, -1, 0, groups, 1, 0, 0),
            (1, -2, half, groups - half, 1, groups, 0),
        ),
        place,
        [data[2], data[-2]],
        [(groups + half, 1), (2 * groups - half, 1)],
        (),
    )
    third = (hop(far[0], 1), hop(far[1], -1))
    recv_second = exchange(near(CHUNKS[2], far_memory([far[0], recv_next])))
    fourth = (hop(third[0][groups:], 1), hop(third[1][groups:], -1))
    recv_far = exchange(join(third, fourth, groups, recv_second))
    *early, back = experts(
        CHUNKS[:3], groups, place, None, (recv_own, recv_next, recv_second), weights
    )
    *late, back = experts(CHUNKS[3:], groups, place, back, (recv_far,), weights)
    x_own, x_oth, s_own, s_oth, hid, gate_grad, up_grad = zip(early, late)
    returned = lax.all_to_all(
        back.reshape(owners, 2 * CAP, HALF), "expert", split_axis=0, concat_axis=0, tiled=True
    )
    theirs = weight_grads(x_oth, s_oth, gate_grad, up_grad, hid, ())
    received = tuple(swap(part) for part in theirs)
    low, high, received = lax.optimization_barrier((*returns(packed, owners), received))
    grads = weight_grads(x_own, s_own, gate_grad, up_grad, hid, received)
    input_grad = combine(low, high, returned.reshape(owners * 2 * CAP, HALF))
    return (input_grad, grads[0][None], grads[1][None], grads[2][None])


def solution(mesh):
    return jax.shard_map(
        local,
        mesh=mesh,
        in_specs=(
            P(("expert", "rep"), None),
            P(("expert", "rep"), None),
            P(("expert", "rep"), None),
            P(("expert", "rep"), None),
            P("expert", "rep", None),
            P("expert", "rep", None),
            P("expert", None, "rep"),
        ),
        out_specs=(
            P(("expert", "rep"), None),
            P("expert", "rep", None),
            P("expert", "rep", None),
            P("expert", None, "rep"),
        ),
        check_vma=False,
    )
```

```python
import functools

import jax
import jax.numpy as jnp
from jax import lax
from jax.experimental import pallas as pl
from jax.experimental.pallas import tpu as pltpu
from jax.sharding import PartitionSpec as P

RING = 8
CAP = 4
META = 128
EXPERT_LIMIT = 40 * 1024 * 1024
HALF = 1024
COLS = 1024
WTILE = 256
CHUNKS = ((0,), (1, -1), (2, -2), (3, -3, 4))
BF = jnp.bfloat16
F32 = jnp.float32
VMEM_LIMIT = 32 * 1024 * 1024
TOKEN_COST = pl.CostEstimate(flops=1, bytes_accessed=1, transcendentals=0)


def far_memory(values):
    return [pltpu.with_memory_space_constraint(value, pltpu.HBM) for value in values]


def dot(a, b, ca, cb):
    return lax.dot_general(a, b, (((ca,), (cb,)), ((), ())), preferred_element_type=F32)


def by_token(columns):
    tokens = columns.shape[0]
    same = lax.broadcasted_iota(jnp.int32, (tokens, tokens), 0) == lax.broadcasted_iota(
        jnp.int32, (tokens, tokens), 1
    )
    return dot(columns, same.astype(F32).astype(BF), 0, 0)


def hits(meta, owner, slot):
    tokens = meta.shape[1]
    first = owner == meta[0:1, :].astype(jnp.int32)
    second = owner == meta[1:2, :].astype(jnp.int32)
    named = (first | second).astype(F32).astype(BF)
    before = (
        lax.broadcasted_iota(jnp.int32, (tokens, tokens), 0)
        < lax.broadcasted_iota(jnp.int32, (tokens, tokens), 1)
    )
    rank = dot(named, before.astype(F32).astype(BF), 1, 0)
    hit = (first | second) & (rank.astype(jnp.int32) == slot)
    gate_first = meta[2:3, :] + meta[3:4, :] + meta[4:5, :]
    gate_second = meta[5:6, :] + meta[6:7, :] + meta[7:8, :]
    gate = jnp.where(first, gate_first, 0.0) + jnp.where(second, gate_second, 0.0)
    return hit, jnp.sum(jnp.where(hit, gate, 0.0), axis=1, keepdims=True)


def pack_kernel(x_ref, grad_ref, ids_ref, gates_ref, out_ref):
    width = x_ref.shape[1]
    tokens = x_ref.shape[0]
    out_ref[:, 0:width] = x_ref[...]
    out_ref[:, width : 2 * width] = grad_ref[...]
    row = lax.broadcasted_iota(jnp.int32, (META, tokens), 0)
    packed = jnp.zeros((META, tokens), F32)
    for k in range(2):
        packed = jnp.where(row == k, ids_ref[k : k + 1, :].astype(F32), packed)
        rest = gates_ref[k : k + 1, :]
        for part in range(3):
            piece = rest.astype(BF).astype(F32)
            packed = jnp.where(row == 2 + 3 * k + part, piece, packed)
            rest = rest - piece
    same = lax.broadcasted_iota(jnp.int32, (tokens, tokens), 0) == lax.broadcasted_iota(
        jnp.int32, (tokens, tokens), 1
    )
    columns = dot(same.astype(F32).astype(BF), packed.astype(BF), 1, 1)
    out_ref[:, 2 * width :] = columns.astype(BF)


def pack(x, grad, ids, gates):
    return pl.pallas_call(
        pack_kernel,
        out_shape=jax.ShapeDtypeStruct((x.shape[0], 2 * x.shape[1] + META), BF),
        compiler_params=pltpu.CompilerParams(vmem_limit_bytes=VMEM_LIMIT),
        cost_estimate=TOKEN_COST,
    )(*far_memory([x, grad, ids, gates]))


def build_kernel(jobs, sources, outs, waits, place_ref, *refs):
    refs = refs[waits:]
    metas, data = refs[:sources], refs[sources : 3 * sources]
    out_refs, picks = refs[3 * sources : 3 * sources + outs], refs[3 * sources + outs :]
    place = place_ref[0]

    @pl.when(pl.program_id(0) == 0)
    def _():
        by = [by_token(meta[...]) for meta in metas]
        for number, (source, offset, start, groups, _, _, _) in enumerate(jobs):
            pick, scale = picks[2 * number], picks[2 * number + 1]
            row = lax.broadcasted_iota(jnp.int32, (groups * 2 * CAP, 128), 0)
            owner = ((row >> 3) + start) * RING + lax.rem(place + offset + RING, RING)
            is_grad = ((row >> 2) & 1) == 1
            hit, gate = hits(by[source], owner, row & 3)
            pick[:, 0:128] = (hit & ~is_grad).astype(F32).astype(BF)
            pick[:, 128:256] = (hit & is_grad).astype(F32).astype(BF)
            scale[...] = jnp.where(is_grad, gate, 1.0)

    for number, (source, _, _, groups, out, to, at) in enumerate(jobs):
        stacked = jnp.concatenate([data[2 * source][...], data[2 * source + 1][...]], axis=0)
        value = dot(picks[2 * number][...], stacked, 1, 0) * picks[2 * number + 1][:, 0:1]
        out_refs[out][to : to + groups, at] = value.astype(BF).reshape(
            groups, 2 * CAP, value.shape[1]
        )


def build(jobs, place, planes, shapes, after=()):
    features = (planes[0].shape[1] - META) // 2
    sources = len(planes)
    tokens = planes[0].shape[0]
    steps = features // COLS
    scratch = []
    for job in jobs:
        rows = job[3] * 2 * CAP
        scratch += [pltpu.VMEM((rows, 256), BF), pltpu.VMEM((rows, 128), F32)]
    shapes = [shape + (2 * CAP,) for shape in shapes]
    return pl.pallas_call(
        functools.partial(build_kernel, jobs, sources, len(shapes), len(after)),
        grid=(steps,),
        out_shape=[pltpu.HBM(shape + (features,), BF) for shape in shapes],
        in_specs=[pl.BlockSpec(memory_space=pltpu.SMEM)]
        + [pl.BlockSpec(memory_space=pl.ANY) for _ in after]
        + [pl.BlockSpec((tokens, META), lambda c: (0, 2 * features // META))] * sources
        + [
            pl.BlockSpec((tokens, COLS), lambda c: (0, c)),
            pl.BlockSpec((tokens, COLS), lambda c: (0, c + steps)),
        ]
        * sources,
        out_specs=[pl.BlockSpec(shape + (COLS,), lambda c: (0, 0, 0, c)) for shape in shapes],
        scratch_shapes=scratch,
        compiler_params=pltpu.CompilerParams(vmem_limit_bytes=VMEM_LIMIT),
        cost_estimate=TOKEN_COST,
    )(place, *after, *planes, *[p for p in planes for _ in range(2)])


def third_kernel(left_ref, right_ref, out_ref):
    out_ref[:, 0:1] = left_ref[...]
    out_ref[:, 1:2] = right_ref[...]


def fourth_kernel(base_ref, left_ref, right_ref, after_ref, out_ref, sems):
    del base_ref, after_ref
    half = left_ref.shape[0]
    copies = [
        pltpu.make_async_copy(left_ref.at[:, 0], out_ref.at[0:half, 2], sems.at[0]),
        pltpu.make_async_copy(right_ref.at[:, 0], out_ref.at[half:, 2], sems.at[1]),
    ]
    for copy in copies:
        copy.start()
    for copy in copies:
        copy.wait()


def join(third, fourth, groups, after):
    features = third[0].shape[3]
    shape = pltpu.HBM((groups, 3, 2 * CAP, features), BF)
    anywhere = pl.BlockSpec(memory_space=pl.ANY)
    base = pl.pallas_call(
        third_kernel,
        grid=(features // COLS,),
        out_shape=shape,
        in_specs=[pl.BlockSpec((groups, 1, 2 * CAP, COLS), lambda c: (0, 0, 0, c))] * 2,
        out_specs=pl.BlockSpec((groups, 2, 2 * CAP, COLS), lambda c: (0, 0, 0, c)),
        compiler_params=pltpu.CompilerParams(vmem_limit_bytes=VMEM_LIMIT),
        cost_estimate=TOKEN_COST,
    )(*third)
    base, after = lax.optimization_barrier((base, after))
    return pl.pallas_call(
        fourth_kernel,
        out_shape=shape,
        in_specs=[anywhere] * 4,
        out_specs=anywhere,
        scratch_shapes=[pltpu.SemaphoreType.DMA((2,))],
        input_output_aliases={0: 0},
        compiler_params=pltpu.CompilerParams(vmem_limit_bytes=VMEM_LIMIT),
        cost_estimate=TOKEN_COST,
    )(*far_memory([base]), *fourth, after)


def expert_kernel(chunks, groups, has_base, place_ref, *refs):
    refs = refs[1:] if has_base else refs
    recvs, refs = refs[: len(chunks)], refs[len(chunks) :]
    sources, results, back = refs[:6], refs[6:13], refs[13]
    held, refs = refs[14:20], refs[20:]
    x_own, x_oth, s_own, s_oth, hid_ref, gg_ref, ug_ref = refs[:7]
    stage, load_sems, store_sems, back_sems = refs[7:]
    wg_own, wg_oth, wu_own, wu_oth, wd_own, wd_oth = held
    place = place_ref[0]
    rep = place_ref[1]
    loads = [
        pltpu.make_async_copy(sources[i], held[i], load_sems.at[i]) for i in range(len(held))
    ]
    stores = [
        pltpu.make_async_copy(refs[i], results[i], store_sems.at[i]) for i in range(len(results))
    ]
    for load in loads:
        load.start()
    start = 0
    for recv, planes in zip(recvs, chunks):
        slots = groups * len(planes) * CAP
        row = lax.broadcasted_iota(jnp.int32, (2 * slots, 2 * slots), 0)
        col = lax.broadcasted_iota(jnp.int32, (2 * slots, 2 * slots), 1)
        grad = (row >= slots).astype(jnp.int32)
        inner = row - slots * grad
        take = (col == (inner >> 2) * 8 + (inner & 3) + 4 * grad).astype(F32).astype(BF)
        for half, x_ref, s_ref in ((rep, x_own, s_own), (1 - rep, x_oth, s_oth)):
            at = pl.ds(pl.multiple_of(half * HALF, HALF), HALF)
            both = dot(take, recv[:, :, :, at].reshape(2 * slots, HALF), 1, 0).astype(BF)
            x_ref[start : start + slots] = both[:slots]
            s_ref[start : start + slots] = both[slots:]
        start += slots
    for store in stores[:4]:
        store.start()
    for load in loads[:2]:
        load.wait()
    gate = dot(x_own[...], wg_own[...], 1, 0) + dot(x_oth[...], wg_oth[...], 1, 0)
    for load in loads[2:4]:
        load.wait()
    up = dot(x_own[...], wu_own[...], 1, 0) + dot(x_oth[...], wu_oth[...], 1, 0)
    sigma = jax.nn.sigmoid(gate)
    silu = gate * sigma
    hid_ref[...] = (silu * up).astype(BF)
    for load in loads[4:]:
        load.wait()
    hidden_grad = dot(s_own[...], wd_own[...], 1, 1) + dot(s_oth[...], wd_oth[...], 1, 1)
    gg_ref[...] = (hidden_grad * up * sigma * (1.0 + gate * (1.0 - sigma))).astype(BF)
    ug_ref[...] = (hidden_grad * silu).astype(BF)
    for store in stores[4:]:
        store.start()
    slot_own = dot(gg_ref[...], wg_own[...], 1, 1) + dot(ug_ref[...], wu_own[...], 1, 1)
    slot_own = slot_own.astype(BF)
    slot_oth = dot(gg_ref[...], wg_oth[...], 1, 1) + dot(ug_ref[...], wu_oth[...], 1, 1)
    slot_oth = slot_oth.astype(BF)
    start = 0
    first = 0
    copies = []
    for planes in chunks:
        count = len(planes)
        slots = groups * count * CAP
        row = lax.broadcasted_iota(jnp.int32, (2 * slots, slots), 0)
        col = lax.broadcasted_iota(jnp.int32, (2 * slots, slots), 1)
        same = ((row >> 3) == (col >> 2)) & ((row & 3) == (col & 3))
        upper = (row >> 2) & 1
        put_own = (same & (upper == rep)).astype(F32).astype(BF)
        put_oth = (same & (upper != rep)).astype(F32).astype(BF)
        mixed = dot(put_own, slot_own[start : start + slots], 1, 0) + dot(
            put_oth, slot_oth[start : start + slots], 1, 0
        )
        stage[:, first : first + count] = mixed.astype(BF).reshape(groups, count, 2 * CAP, HALF)
        for index, plane in enumerate(planes):
            copy = pltpu.make_async_copy(
                stage.at[:, first + index],
                back.at[:, lax.rem(place - plane + RING, RING)],
                back_sems.at[first + index],
            )
            copy.start()
            copies.append(copy)
        start += slots
        first += count
    for copy in copies + stores:
        copy.wait()


def experts(chunks, groups, place, base, recvs, weights):
    planes = sum(len(chunk) for chunk in chunks)
    slots = groups * planes * CAP
    hidden = weights[0].shape[1]
    has_base = base is not None
    bases = far_memory([base]) if has_base else []
    anywhere = pl.BlockSpec(memory_space=pl.ANY)
    return pl.pallas_call(
        functools.partial(expert_kernel, chunks, groups, has_base),
        out_shape=(
            [pltpu.HBM((slots, HALF), BF)] * 4
            + [pltpu.HBM((slots, hidden), BF)] * 3
            + [pltpu.HBM((groups, RING, 2 * CAP, HALF), BF)]
        ),
        in_specs=[pl.BlockSpec(memory_space=pltpu.SMEM)]
        + [anywhere for _ in bases]
        + [pl.BlockSpec(memory_space=pltpu.VMEM) for _ in recvs]
        + [anywhere] * 6,
        out_specs=[anywhere] * 8,
        scratch_shapes=[pltpu.VMEM(w.shape, BF) for w in weights]
        + [pltpu.VMEM((slots, HALF), BF)] * 4
        + [pltpu.VMEM((slots, hidden), BF)] * 3
        + [
            pltpu.VMEM((groups, planes, 2 * CAP, HALF), BF),
            pltpu.SemaphoreType.DMA((6,)),
            pltpu.SemaphoreType.DMA((7,)),
            pltpu.SemaphoreType.DMA((planes,)),
        ],
        input_output_aliases={1: 7} if has_base else {},
        compiler_params=pltpu.CompilerParams(vmem_limit_bytes=EXPERT_LIMIT),
        cost_estimate=TOKEN_COST,
    )(place, *bases, *recvs, *far_memory(weights))


def weight_kernel(parts, has_sum, *refs):
    xs, ss, gates, ups, hids = (refs[i * parts : (i + 1) * parts] for i in range(5))
    rest = refs[5 * parts :]
    outs = rest[-3:]

    def total(left, right):
        value = dot(left[0][...], right[0][...], 0, 0)
        for i in range(1, parts):
            value += dot(left[i][...], right[i][...], 0, 0)
        return value.astype(BF)

    for index, (left, right) in enumerate(((xs, gates), (xs, ups), (hids, ss))):
        part = total(left, right)
        if has_sum:
            part = (part.astype(F32) + rest[index][...].astype(F32)).astype(BF)
        outs[index][...] = part


def weight_grads(xs, ss, gates, ups, hids, received):
    hidden = gates[0].shape[1]
    wide = pl.BlockSpec((WTILE, hidden), lambda c: (c, 0))
    tall = pl.BlockSpec((hidden, WTILE), lambda c: (0, c))
    part_specs = [wide, wide, tall]
    narrow = [*xs, *ss]
    whole = [*gates, *ups, *hids]
    return pl.pallas_call(
        functools.partial(weight_kernel, len(xs), bool(received)),
        grid=(HALF // WTILE,),
        out_shape=[
            pltpu.HBM((HALF, hidden), BF),
            pltpu.HBM((HALF, hidden), BF),
            pltpu.HBM((hidden, HALF), BF),
        ],
        in_specs=[pl.BlockSpec((v.shape[0], WTILE), lambda c: (0, c)) for v in narrow]
        + [pl.BlockSpec(v.shape, lambda c: (0, 0)) for v in whole]
        + (part_specs if received else []),
        out_specs=part_specs,
        compiler_params=pltpu.CompilerParams(vmem_limit_bytes=VMEM_LIMIT),
        cost_estimate=TOKEN_COST,
    )(*far_memory([*narrow, *whole]), *received)


def returns_kernel(meta_ref, low_ref, high_ref):
    rows = low_ref.shape[0]
    row = lax.broadcasted_iota(jnp.int32, (rows, 128), 0)
    hit, _ = hits(by_token(meta_ref[...]), row >> 3, row & 3)
    upper = ((row >> 2) & 1) == 1
    low_ref[...] = (hit & ~upper).astype(F32).astype(BF)
    high_ref[...] = (hit & upper).astype(F32).astype(BF)


def returns(packed, owners):
    rows = owners * 2 * CAP
    whole = pl.BlockSpec((rows, 128), lambda c: (0, 0))
    return pl.pallas_call(
        returns_kernel,
        grid=(1,),
        out_shape=[jax.ShapeDtypeStruct((rows, 128), BF)] * 2,
        in_specs=[pl.BlockSpec((128, META), lambda c: (0, 4 * HALF // META))],
        out_specs=[whole, whole],
        compiler_params=pltpu.CompilerParams(vmem_limit_bytes=VMEM_LIMIT),
        cost_estimate=TOKEN_COST,
    )(packed)


def combine_kernel(low_ref, high_ref, back_ref, out_ref):
    out_ref[:, 0:HALF] = dot(low_ref[...], back_ref[...], 0, 0).astype(BF)
    out_ref[:, HALF : 2 * HALF] = dot(high_ref[...], back_ref[...], 0, 0).astype(BF)


def combine(low, high, back):
    return pl.pallas_call(
        combine_kernel,
        out_shape=jax.ShapeDtypeStruct((128, 2 * HALF), BF),
        compiler_params=pltpu.CompilerParams(vmem_limit_bytes=VMEM_LIMIT),
        cost_estimate=TOKEN_COST,
    )(low, high, back)


def local(inputs, out_grad, expert_ids, gates, gate_w, up_w, down_w):
    owners = lax.axis_size("expert")
    groups = owners // RING
    across = [[g * RING + z for g in range(groups)] for z in range(RING)]
    place = jnp.stack(
        [lax.rem(lax.axis_index("expert"), RING), lax.axis_index("rep")]
    ).astype(jnp.int32)

    def hop(value, by):
        pairs = [(g * RING + z, g * RING + (z + by) % RING) for g in range(groups) for z in range(RING)]
        return lax.ppermute(value, "expert", pairs)

    def swap(value):
        return lax.ppermute(value, "rep", [(0, 1), (1, 0)])

    packed = pack(inputs, out_grad, expert_ids.T, gates.T)
    data = {0: packed, 1: hop(packed, 1), -1: hop(packed, -1)}
    own = (gate_w[0], up_w[0], down_w[0])
    oth = tuple(swap(w) for w in own)
    weights = (own[0], oth[0], own[1], oth[1], own[2], oth[2])

    def near(planes, after):
        jobs = tuple((i, 0, 0, groups, 0, 0, i) for i in range(len(planes)))
        (sent,) = build(
            jobs,
            place,
            far_memory([data[p] for p in planes]) if planes == CHUNKS[1] else [data[p] for p in planes],
            [(groups, len(planes))],
            after,
        )
        return sent

    def exchange(sent):
        return lax.all_to_all(
            sent, "expert", split_axis=0, concat_axis=0, tiled=True, axis_index_groups=across
        )

    recv_own = exchange(near(CHUNKS[0], ()))
    recv_own, data[1], data[-1] = lax.optimization_barrier((recv_own, data[1], data[-1]))
    for by in (1, -1):
        data[2 * by] = hop(data[by], by)
    recv_next = exchange(near(CHUNKS[1], ()))
    half = groups // 2
    far = build(
        (
            (0, 1, 0, groups, 0, 0, 0),
            (0, 2, 0, half, 0, groups, 0),
            (1, -1, 0, groups, 1, 0, 0),
            (1, -2, half, groups - half, 1, groups, 0),
        ),
        place,
        [data[2], data[-2]],
        [(groups + half, 1), (2 * groups - half, 1)],
        (),
    )
    third = (hop(far[0], 1), hop(far[1], -1))
    recv_second = exchange(near(CHUNKS[2], far_memory([far[0], recv_next])))
    fourth = (hop(third[0][groups:], 1), hop(third[1][groups:], -1))
    recv_far = exchange(join(third, fourth, groups, recv_second))
    *early, back = experts(
        CHUNKS[:3], groups, place, None, (recv_own, recv_next, recv_second), weights
    )
    *late, back = experts(CHUNKS[3:], groups, place, back, (recv_far,), weights)
    x_own, x_oth, s_own, s_oth, hid, gate_grad, up_grad = zip(early, late)
    returned = lax.all_to_all(
        back.reshape(owners, 2 * CAP, HALF), "expert", split_axis=0, concat_axis=0, tiled=True
    )
    theirs = weight_grads(x_oth, s_oth, gate_grad, up_grad, hid, ())
    received = tuple(swap(part) for part in theirs)
    low, high, received = lax.optimization_barrier((*returns(packed, owners), received))
    grads = weight_grads(x_own, s_own, gate_grad, up_grad, hid, received)
    input_grad = combine(low, high, returned.reshape(owners * 2 * CAP, HALF))
    return (input_grad, grads[0][None], grads[1][None], grads[2][None])


def solution(mesh):
    return jax.shard_map(
        local,
        mesh=mesh,
        in_specs=(
            P(("expert", "rep"), None),
            P(("expert", "rep"), None),
            P(("expert", "rep"), None),
            P(("expert", "rep"), None),
            P("expert", "rep", None),
            P("expert", "rep", None),
            P("expert", None, "rep"),
        ),
        out_specs=(
            P(("expert", "rep"), None),
            P("expert", "rep", None),
            P("expert", "rep", None),
            P("expert", None, "rep"),
        ),
        check_vma=False,
    )
```

```python
import functools

import jax
import jax.numpy as jnp
from jax import lax
from jax.experimental import pallas as pl
from jax.experimental.pallas import tpu as pltpu
from jax.sharding import PartitionSpec as P

RING = 8
CAP = 4
META = 128
EXPERT_LIMIT = 40 * 1024 * 1024
BESIDE_LIMIT = 60 * 1024 * 1024
HALF = 1024
COLS = 1024
WTILE = 256
CHUNKS = ((0,), (1, -1), (2, -2), (3, -3, 4))
BF = jnp.bfloat16
F32 = jnp.float32
VMEM_LIMIT = 32 * 1024 * 1024
TOKEN_COST = pl.CostEstimate(flops=1, bytes_accessed=1, transcendentals=0)


def far_memory(values):
    return [pltpu.with_memory_space_constraint(value, pltpu.HBM) for value in values]


def dot(a, b, ca, cb):
    return lax.dot_general(a, b, (((ca,), (cb,)), ((), ())), preferred_element_type=F32)


def by_token(columns):
    tokens = columns.shape[0]
    same = lax.broadcasted_iota(jnp.int32, (tokens, tokens), 0) == lax.broadcasted_iota(
        jnp.int32, (tokens, tokens), 1
    )
    return dot(columns, same.astype(F32).astype(BF), 0, 0)


def hits(meta, owner, slot):
    tokens = meta.shape[1]
    first = owner == meta[0:1, :].astype(jnp.int32)
    second = owner == meta[1:2, :].astype(jnp.int32)
    named = (first | second).astype(F32).astype(BF)
    before = (
        lax.broadcasted_iota(jnp.int32, (tokens, tokens), 0)
        < lax.broadcasted_iota(jnp.int32, (tokens, tokens), 1)
    )
    rank = dot(named, before.astype(F32).astype(BF), 1, 0)
    hit = (first | second) & (rank.astype(jnp.int32) == slot)
    gate_first = meta[2:3, :] + meta[3:4, :] + meta[4:5, :]
    gate_second = meta[5:6, :] + meta[6:7, :] + meta[7:8, :]
    gate = jnp.where(first, gate_first, 0.0) + jnp.where(second, gate_second, 0.0)
    return hit, jnp.sum(jnp.where(hit, gate, 0.0), axis=1, keepdims=True)


def pack_kernel(x_ref, grad_ref, ids_ref, gates_ref, out_ref):
    width = x_ref.shape[1]
    tokens = x_ref.shape[0]
    out_ref[:, 0:width] = x_ref[...]
    out_ref[:, width : 2 * width] = grad_ref[...]
    row = lax.broadcasted_iota(jnp.int32, (META, tokens), 0)
    packed = jnp.zeros((META, tokens), F32)
    for k in range(2):
        packed = jnp.where(row == k, ids_ref[k : k + 1, :].astype(F32), packed)
        rest = gates_ref[k : k + 1, :]
        for part in range(3):
            piece = rest.astype(BF).astype(F32)
            packed = jnp.where(row == 2 + 3 * k + part, piece, packed)
            rest = rest - piece
    same = lax.broadcasted_iota(jnp.int32, (tokens, tokens), 0) == lax.broadcasted_iota(
        jnp.int32, (tokens, tokens), 1
    )
    columns = dot(same.astype(F32).astype(BF), packed.astype(BF), 1, 1)
    out_ref[:, 2 * width :] = columns.astype(BF)


def pack(x, grad, ids, gates):
    return pl.pallas_call(
        pack_kernel,
        out_shape=jax.ShapeDtypeStruct((x.shape[0], 2 * x.shape[1] + META), BF),
        compiler_params=pltpu.CompilerParams(vmem_limit_bytes=VMEM_LIMIT),
        cost_estimate=TOKEN_COST,
    )(*far_memory([x, grad, ids, gates]))


def build_kernel(jobs, sources, outs, waits, place_ref, *refs):
    refs = refs[waits:]
    metas, data = refs[:sources], refs[sources : 3 * sources]
    out_refs, picks = refs[3 * sources : 3 * sources + outs], refs[3 * sources + outs :]
    place = place_ref[0]

    @pl.when(pl.program_id(0) == 0)
    def _():
        by = [by_token(meta[...]) for meta in metas]
        for number, (source, offset, start, groups, _, _, _) in enumerate(jobs):
            pick, scale = picks[2 * number], picks[2 * number + 1]
            row = lax.broadcasted_iota(jnp.int32, (groups * 2 * CAP, 128), 0)
            owner = ((row >> 3) + start) * RING + lax.rem(place + offset + RING, RING)
            is_grad = ((row >> 2) & 1) == 1
            hit, gate = hits(by[source], owner, row & 3)
            pick[:, 0:128] = (hit & ~is_grad).astype(F32).astype(BF)
            pick[:, 128:256] = (hit & is_grad).astype(F32).astype(BF)
            scale[...] = jnp.where(is_grad, gate, 1.0)

    for number, (source, _, _, groups, out, to, at) in enumerate(jobs):
        stacked = jnp.concatenate([data[2 * source][...], data[2 * source + 1][...]], axis=0)
        value = dot(picks[2 * number][...], stacked, 1, 0) * picks[2 * number + 1][:, 0:1]
        out_refs[out][to : to + groups, at] = value.astype(BF).reshape(
            groups, 2 * CAP, value.shape[1]
        )


def build(jobs, place, planes, shapes, after=(), limit=VMEM_LIMIT):
    features = (planes[0].shape[1] - META) // 2
    sources = len(planes)
    tokens = planes[0].shape[0]
    steps = features // COLS
    scratch = []
    for job in jobs:
        rows = job[3] * 2 * CAP
        scratch += [pltpu.VMEM((rows, 256), BF), pltpu.VMEM((rows, 128), F32)]
    shapes = [shape + (2 * CAP,) for shape in shapes]
    return pl.pallas_call(
        functools.partial(build_kernel, jobs, sources, len(shapes), len(after)),
        grid=(steps,),
        out_shape=[pltpu.HBM(shape + (features,), BF) for shape in shapes],
        in_specs=[pl.BlockSpec(memory_space=pltpu.SMEM)]
        + [pl.BlockSpec(memory_space=pl.ANY) for _ in after]
        + [pl.BlockSpec((tokens, META), lambda c: (0, 2 * features // META))] * sources
        + [
            pl.BlockSpec((tokens, COLS), lambda c: (0, c)),
            pl.BlockSpec((tokens, COLS), lambda c: (0, c + steps)),
        ]
        * sources,
        out_specs=[pl.BlockSpec(shape + (COLS,), lambda c: (0, 0, 0, c)) for shape in shapes],
        scratch_shapes=scratch,
        compiler_params=pltpu.CompilerParams(vmem_limit_bytes=limit),
        cost_estimate=TOKEN_COST,
    )(place, *after, *planes, *[p for p in planes for _ in range(2)])


def join_kernel(left_ref, right_ref, far_left_ref, far_right_ref, after_ref, out_ref):
    del after_ref
    half = far_left_ref.shape[0]
    out_ref[:, 0:1] = left_ref[...]
    out_ref[:, 1:2] = right_ref[...]
    out_ref[0:half, 2:3] = far_left_ref[...]
    out_ref[half:, 2:3] = far_right_ref[...]


def join(third, fourth, groups, after):
    features = third[0].shape[3]
    shape = (groups, 1, 2 * CAP)
    specs = [pl.BlockSpec(shape + (COLS,), lambda c: (0, 0, 0, c))] * 2
    specs += [pl.BlockSpec(v.shape[:3] + (COLS,), lambda c: (0, 0, 0, c)) for v in fourth]
    return pl.pallas_call(
        join_kernel,
        grid=(features // COLS,),
        out_shape=pltpu.HBM((groups, 3, 2 * CAP, features), BF),
        in_specs=specs + [pl.BlockSpec(memory_space=pl.ANY)],
        out_specs=pl.BlockSpec((groups, 3, 2 * CAP, COLS), lambda c: (0, 0, 0, c)),
        compiler_params=pltpu.CompilerParams(vmem_limit_bytes=VMEM_LIMIT),
        cost_estimate=TOKEN_COST,
    )(*third, *fourth, after)


def expert_kernel(chunks, groups, has_base, place_ref, *refs):
    refs = refs[1:] if has_base else refs
    arrived, refs = refs[: len(chunks)], refs[len(chunks) :]
    sources, results, back = refs[:6], refs[6:13], refs[13]
    held, refs = refs[14:20], refs[20:]
    recvs, refs = refs[: len(chunks)], refs[len(chunks) :]
    x_own, x_oth, s_own, s_oth, hid_ref, gg_ref, ug_ref = refs[:7]
    stage, load_sems, store_sems, back_sems, recv_sems = refs[7:]
    wg_own, wg_oth, wu_own, wu_oth, wd_own, wd_oth = held
    place = place_ref[0]
    rep = place_ref[1]
    loads = [
        pltpu.make_async_copy(sources[i], held[i], load_sems.at[i]) for i in range(len(held))
    ]
    stores = [
        pltpu.make_async_copy(refs[i], results[i], store_sems.at[i]) for i in range(len(results))
    ]
    takes = [
        pltpu.make_async_copy(arrived[i], recvs[i], recv_sems.at[i]) for i in range(len(recvs))
    ]
    for copy in takes + loads:
        copy.start()
    start = 0
    for copy, recv, planes in zip(takes, recvs, chunks):
        copy.wait()
        slots = groups * len(planes) * CAP
        row = lax.broadcasted_iota(jnp.int32, (2 * slots, 2 * slots), 0)
        col = lax.broadcasted_iota(jnp.int32, (2 * slots, 2 * slots), 1)
        grad = (row >= slots).astype(jnp.int32)
        inner = row - slots * grad
        take = (col == (inner >> 2) * 8 + (inner & 3) + 4 * grad).astype(F32).astype(BF)
        for half, x_ref, s_ref in ((rep, x_own, s_own), (1 - rep, x_oth, s_oth)):
            at = pl.ds(pl.multiple_of(half * HALF, HALF), HALF)
            both = dot(take, recv[:, :, :, at].reshape(2 * slots, HALF), 1, 0).astype(BF)
            x_ref[start : start + slots] = both[:slots]
            s_ref[start : start + slots] = both[slots:]
        start += slots
    for store in stores[:4]:
        store.start()
    for load in loads[:2]:
        load.wait()
    gate = dot(x_own[...], wg_own[...], 1, 0) + dot(x_oth[...], wg_oth[...], 1, 0)
    for load in loads[2:4]:
        load.wait()
    up = dot(x_own[...], wu_own[...], 1, 0) + dot(x_oth[...], wu_oth[...], 1, 0)
    sigma = jax.nn.sigmoid(gate)
    silu = gate * sigma
    hid_ref[...] = (silu * up).astype(BF)
    for load in loads[4:]:
        load.wait()
    hidden_grad = dot(s_own[...], wd_own[...], 1, 1) + dot(s_oth[...], wd_oth[...], 1, 1)
    gg_ref[...] = (hidden_grad * up * sigma * (1.0 + gate * (1.0 - sigma))).astype(BF)
    ug_ref[...] = (hidden_grad * silu).astype(BF)
    for store in stores[4:]:
        store.start()
    slot_own = dot(gg_ref[...], wg_own[...], 1, 1) + dot(ug_ref[...], wu_own[...], 1, 1)
    slot_own = slot_own.astype(BF)
    slot_oth = dot(gg_ref[...], wg_oth[...], 1, 1) + dot(ug_ref[...], wu_oth[...], 1, 1)
    slot_oth = slot_oth.astype(BF)
    start = 0
    first = 0
    copies = []
    for planes in chunks:
        count = len(planes)
        slots = groups * count * CAP
        row = lax.broadcasted_iota(jnp.int32, (2 * slots, slots), 0)
        col = lax.broadcasted_iota(jnp.int32, (2 * slots, slots), 1)
        same = ((row >> 3) == (col >> 2)) & ((row & 3) == (col & 3))
        upper = (row >> 2) & 1
        put_own = (same & (upper == rep)).astype(F32).astype(BF)
        put_oth = (same & (upper != rep)).astype(F32).astype(BF)
        mixed = dot(put_own, slot_own[start : start + slots], 1, 0) + dot(
            put_oth, slot_oth[start : start + slots], 1, 0
        )
        stage[:, first : first + count] = mixed.astype(BF).reshape(groups, count, 2 * CAP, HALF)
        for index, plane in enumerate(planes):
            copy = pltpu.make_async_copy(
                stage.at[:, first + index],
                back.at[:, lax.rem(place - plane + RING, RING)],
                back_sems.at[first + index],
            )
            copy.start()
            copies.append(copy)
        start += slots
        first += count
    for copy in copies + stores:
        copy.wait()


def experts(chunks, groups, place, base, recvs, weights):
    planes = sum(len(chunk) for chunk in chunks)
    slots = groups * planes * CAP
    hidden = weights[0].shape[1]
    has_base = base is not None
    bases = far_memory([base]) if has_base else []
    anywhere = pl.BlockSpec(memory_space=pl.ANY)
    return pl.pallas_call(
        functools.partial(expert_kernel, chunks, groups, has_base),
        out_shape=(
            [pltpu.HBM((slots, HALF), BF)] * 4
            + [pltpu.HBM((slots, hidden), BF)] * 3
            + [pltpu.HBM((groups, RING, 2 * CAP, HALF), BF)]
        ),
        in_specs=[pl.BlockSpec(memory_space=pltpu.SMEM)]
        + [anywhere for _ in bases]
        + [anywhere for _ in recvs]
        + [anywhere] * 6,
        out_specs=[anywhere] * 8,
        scratch_shapes=[pltpu.VMEM(v.shape, BF) for v in (*weights, *recvs)]
        + [pltpu.VMEM((slots, HALF), BF)] * 4
        + [pltpu.VMEM((slots, hidden), BF)] * 3
        + [
            pltpu.VMEM((groups, planes, 2 * CAP, HALF), BF),
            pltpu.SemaphoreType.DMA((6,)),
            pltpu.SemaphoreType.DMA((7,)),
            pltpu.SemaphoreType.DMA((planes,)),
            pltpu.SemaphoreType.DMA((len(recvs),)),
        ],
        input_output_aliases={1: 7} if has_base else {},
        compiler_params=pltpu.CompilerParams(vmem_limit_bytes=EXPERT_LIMIT),
        cost_estimate=TOKEN_COST,
    )(place, *bases, *recvs, *far_memory(weights))


def weight_kernel(parts, has_sum, *refs):
    xs, ss, gates, ups, hids = (refs[i * parts : (i + 1) * parts] for i in range(5))
    rest = refs[5 * parts :]
    outs = rest[-3:]

    def total(left, right):
        value = dot(left[0][...], right[0][...], 0, 0)
        for i in range(1, parts):
            value += dot(left[i][...], right[i][...], 0, 0)
        return value.astype(BF)

    for index, (left, right) in enumerate(((xs, gates), (xs, ups), (hids, ss))):
        part = total(left, right)
        if has_sum:
            part = (part.astype(F32) + rest[index][...].astype(F32)).astype(BF)
        outs[index][...] = part


def weight_grads(xs, ss, gates, ups, hids, received):
    hidden = gates[0].shape[1]
    wide = pl.BlockSpec((WTILE, hidden), lambda c: (c, 0))
    tall = pl.BlockSpec((hidden, WTILE), lambda c: (0, c))
    part_specs = [wide, wide, tall]
    narrow = [*xs, *ss]
    whole = [*gates, *ups, *hids]
    return pl.pallas_call(
        functools.partial(weight_kernel, len(xs), bool(received)),
        grid=(HALF // WTILE,),
        out_shape=[
            pltpu.HBM((HALF, hidden), BF),
            pltpu.HBM((HALF, hidden), BF),
            pltpu.HBM((hidden, HALF), BF),
        ],
        in_specs=[pl.BlockSpec((v.shape[0], WTILE), lambda c: (0, c)) for v in narrow]
        + [pl.BlockSpec(v.shape, lambda c: (0, 0)) for v in whole]
        + (part_specs if received else []),
        out_specs=part_specs,
        compiler_params=pltpu.CompilerParams(vmem_limit_bytes=VMEM_LIMIT),
        cost_estimate=TOKEN_COST,
    )(*far_memory([*narrow, *whole]), *received)


def returns_kernel(meta_ref, low_ref, high_ref):
    rows = low_ref.shape[0]
    row = lax.broadcasted_iota(jnp.int32, (rows, 128), 0)
    hit, _ = hits(by_token(meta_ref[...]), row >> 3, row & 3)
    upper = ((row >> 2) & 1) == 1
    low_ref[...] = (hit & ~upper).astype(F32).astype(BF)
    high_ref[...] = (hit & upper).astype(F32).astype(BF)


def returns(packed, owners):
    rows = owners * 2 * CAP
    whole = pl.BlockSpec((rows, 128), lambda c: (0, 0))
    return pl.pallas_call(
        returns_kernel,
        grid=(1,),
        out_shape=[jax.ShapeDtypeStruct((rows, 128), BF)] * 2,
        in_specs=[pl.BlockSpec((128, META), lambda c: (0, 4 * HALF // META))],
        out_specs=[whole, whole],
        compiler_params=pltpu.CompilerParams(vmem_limit_bytes=VMEM_LIMIT),
        cost_estimate=TOKEN_COST,
    )(packed)


def combine_kernel(low_ref, high_ref, back_ref, out_ref):
    out_ref[:, 0:HALF] = dot(low_ref[...], back_ref[...], 0, 0).astype(BF)
    out_ref[:, HALF : 2 * HALF] = dot(high_ref[...], back_ref[...], 0, 0).astype(BF)


def combine(low, high, back):
    return pl.pallas_call(
        combine_kernel,
        out_shape=jax.ShapeDtypeStruct((128, 2 * HALF), BF),
        compiler_params=pltpu.CompilerParams(vmem_limit_bytes=VMEM_LIMIT),
        cost_estimate=TOKEN_COST,
    )(low, high, back)


def local(inputs, out_grad, expert_ids, gates, gate_w, up_w, down_w):
    owners = lax.axis_size("expert")
    groups = owners // RING
    across = [[g * RING + z for g in range(groups)] for z in range(RING)]
    place = jnp.stack(
        [lax.rem(lax.axis_index("expert"), RING), lax.axis_index("rep")]
    ).astype(jnp.int32)

    def hop(value, by):
        pairs = [(g * RING + z, g * RING + (z + by) % RING) for g in range(groups) for z in range(RING)]
        return lax.ppermute(value, "expert", pairs)

    def swap(value):
        return lax.ppermute(value, "rep", [(0, 1), (1, 0)])

    packed = pack(inputs, out_grad, expert_ids.T, gates.T)
    data = {0: packed, 1: hop(packed, 1), -1: hop(packed, -1)}
    own = (gate_w[0], up_w[0], down_w[0])
    oth = tuple(swap(w) for w in own)
    weights = (own[0], oth[0], own[1], oth[1], own[2], oth[2])

    def near(planes, after):
        jobs = tuple((i, 0, 0, groups, 0, 0, i) for i in range(len(planes)))
        (sent,) = build(
            jobs,
            place,
            far_memory([data[p] for p in planes]) if planes == CHUNKS[1] else [data[p] for p in planes],
            [(groups, len(planes))],
            after,
            BESIDE_LIMIT if planes == CHUNKS[0] else VMEM_LIMIT,
        )
        return sent

    def exchange(sent):
        return lax.all_to_all(
            sent, "expert", split_axis=0, concat_axis=0, tiled=True, axis_index_groups=across
        )

    recv_own = exchange(near(CHUNKS[0], ()))
    recv_own, data[1], data[-1] = lax.optimization_barrier((recv_own, data[1], data[-1]))
    for by in (1, -1):
        data[2 * by] = hop(data[by], by)
    recv_next = exchange(near(CHUNKS[1], ()))
    half = groups // 2
    far = build(
        (
            (0, 1, 0, groups, 0, 0, 0),
            (0, 2, 0, half, 0, groups, 0),
            (1, -1, 0, groups, 1, 0, 0),
            (1, -2, half, groups - half, 1, groups, 0),
        ),
        place,
        [data[2], data[-2]],
        [(groups + half, 1), (2 * groups - half, 1)],
        (),
    )
    third = (hop(far[0], 1), hop(far[1], -1))
    recv_second = exchange(near(CHUNKS[2], [*far_memory([far[0]]), recv_next]))
    fourth = (hop(third[0][groups:], 1), hop(third[1][groups:], -1))
    recv_far = exchange(join(third, fourth, groups, recv_second))
    *early, back = experts(
        CHUNKS[:3], groups, place, None, (recv_own, recv_next, recv_second), weights
    )
    *late, back = experts(CHUNKS[3:], groups, place, back, (recv_far,), weights)
    x_own, x_oth, s_own, s_oth, hid, gate_grad, up_grad = zip(early, late)
    returned = lax.all_to_all(
        back.reshape(owners, 2 * CAP, HALF), "expert", split_axis=0, concat_axis=0, tiled=True
    )
    theirs = weight_grads(x_oth, s_oth, gate_grad, up_grad, hid, ())
    received = tuple(swap(part) for part in theirs)
    low, high, received = lax.optimization_barrier((*returns(packed, owners), received))
    grads = weight_grads(x_own, s_own, gate_grad, up_grad, hid, received)
    input_grad = combine(low, high, returned.reshape(owners * 2 * CAP, HALF))
    return (input_grad, grads[0][None], grads[1][None], grads[2][None])


def solution(mesh):
    return jax.shard_map(
        local,
        mesh=mesh,
        in_specs=(
            P(("expert", "rep"), None),
            P(("expert", "rep"), None),
            P(("expert", "rep"), None),
            P(("expert", "rep"), None),
            P("expert", "rep", None),
            P("expert", "rep", None),
            P("expert", None, "rep"),
        ),
        out_specs=(
            P(("expert", "rep"), None),
            P("expert", "rep", None),
            P("expert", "rep", None),
            P("expert", None, "rep"),
        ),
        check_vma=False,
    )
```
